256 devices in a mesh: region: 32 (over y, x, core), block: 8 (over z).
Axes of the slice: x: 4, y: 4, z: 8, core: 2. Of those that a mesh axis runs over, the one named last changes fastest.
Arguments:
- right_side: float32 [768, 512, 256], P('region', 'block'), may hold values from -6 to 6
- knudsen: float32 [768, 512, 256], P('region', 'block'), may hold values from 0.1 to 1
- solid: int32 [768, 512, 256], P('region', 'block'), may hold values 0 or 1
Outputs:
- concentration: float32 [768, 512, 256], P('region', 'block')
The draws below stay inside these ranges and needn't reach their ends.
Inputs may be any that keep to these rules, and one draw needn't show every extreme that they name: 1 marks a solid voxel, 0 a pore.
All inputs are finite; a program needn't handle non-finite values. No bound on the sum of `solid` on one device may be relied on, other than what follows from the above.
Results may differ from the reference program's by a relative error of at most 0.00002.
Values sent between devices are 32-bit elements; how exact they have to be, the bound alone decides.
A program may use at most 128 MiB of HBM per device.

```python
import math
import jax
import jax.numpy as jnp

COARSEN = 8
PRE_SWEEPS = 3
POST_SWEEPS = 3
COARSE_SWEEPS = 6
NX = 768
NY = 512
NZ = 256


def with_ends(array, key, low, largest):
    longest = array.shape.index(max(array.shape))
    spots = []
    for shift in (0, 1):
        where = [jax.random.randint(jax.random.fold_in(key, axis), (), 0, length) for axis, length in enumerate(array.shape)]
        where[longest] = (where[longest] + shift) % array.shape[longest]
        spots.append(tuple(where))
    return array.at[spots[0]].set(low).at[spots[1]].set(largest)


def steps_of(key, shape, pieces, least, largest):
    gain = 1.0
    for dim, shards_of in pieces:
        steps = jax.random.uniform(jax.random.fold_in(jax.random.fold_in(key, 6), dim), (shards_of,), jnp.float32, least / len(pieces), largest / len(pieces))
        gain = gain * jnp.repeat(jnp.exp(steps), shape[dim] // shards_of).reshape((-1,) + (1,) * (len(shape) - 1 - dim))
    return gain


def gaussian(stream_key, extent, scale, reach, split=(), dtype=jnp.bfloat16):
    result = scale * jax.random.normal(stream_key, extent, jnp.float32)
    if split:
        result = result * steps_of(stream_key, extent, split, -0.22, 0.18)
    return jnp.clip(result, -reach, reach).astype(dtype)


def setup_inputs(seed: int = 0) -> dict:
    splits = jax.random.split(jax.random.key(seed), 4)
    right_side = gaussian(splits[0], (NX, NY, NZ), 1.0, 6.0, ((0, 32), (1, 8)), jnp.float32)
    knudsen = jnp.clip(jnp.exp(math.log(1.0) - 2.3025851 * jax.random.uniform(splits[1], (NX, NY, NZ), jnp.float32) ** steps_of(splits[1], (NX, NY, NZ), ((0, 32), (1, 8)), -0.2, 0.2)), 0.1, 1.0)
    solid = with_ends((jax.random.randint(splits[2], (NX, NY, NZ), 0, 4) < 1).astype(jnp.int32), jax.random.fold_in(splits[2], 1), 0, 1)
    return dict(right_side=right_side, knudsen=knudsen, solid=solid)


MASS_TERM = 0.05
RELAX_WEIGHT = 0.8

def neighbours(padded):
    center = padded[1:-1, 1:-1, :]
    along_z = jnp.pad(center, ((0, 0), (0, 0), (1, 1)))
    total = padded[2:, 1:-1, :] + padded[:-2, 1:-1, :]
    total = total + padded[1:-1, 2:, :] + padded[1:-1, :-2, :]
    return total + along_z[:, :, 2:] + along_z[:, :, :-2]

def aggregate(values):
    dims = values.shape
    shaped = values.reshape(dims[0] // COARSEN, COARSEN, dims[1] // COARSEN, COARSEN, dims[2] // COARSEN, COARSEN)
    return shaped.sum(axis=(1, 3, 5))

def coarse_operator(coef_pad, pore_mask, residual):
    dims = pore_mask.shape
    inner = coef_pad[1:-1, 1:-1, :]
    face_x = (coef_pad[1:, 1:-1, :] * coef_pad[:-1, 1:-1, :])[::COARSEN]
    cond_x = face_x.reshape(face_x.shape[0], dims[1] // COARSEN, COARSEN, dims[2] // COARSEN, COARSEN).sum(axis=(2, 4))
    face_y = (coef_pad[1:-1, 1:, :] * coef_pad[1:-1, :-1, :])[:, ::COARSEN]
    cond_y = face_y.reshape(dims[0] // COARSEN, COARSEN, face_y.shape[1], dims[2] // COARSEN, COARSEN).sum(axis=(1, 4))
    padded_z = jnp.pad(inner, ((0, 0), (0, 0), (1, 1)))
    face_z = (padded_z[:, :, 1:] * padded_z[:, :, :-1])[:, :, ::COARSEN]
    cond_z = face_z.reshape(dims[0] // COARSEN, COARSEN, dims[1] // COARSEN, COARSEN, face_z.shape[2]).sum(axis=(1, 3))
    count = aggregate(pore_mask)
    coarse_residual = aggregate(residual)
    coarse_diag = MASS_TERM * (count + 1.0) + cond_x[:-1] + cond_x[1:] + cond_y[:, :-1] + cond_y[:, 1:] + cond_z[:, :, :-1] + cond_z[:, :, 1:]
    return jnp.stack([coarse_residual, coarse_diag, cond_x[:-1], cond_x[1:], cond_y[:, :-1], cond_y[:, 1:], cond_z[:, :, :-1], cond_z[:, :, 1:]])

def coarse_relax(stacked, pad_coarse):
    coarse_residual = stacked[0]
    coarse_diag = stacked[1]
    correction = RELAX_WEIGHT * coarse_residual / coarse_diag
    for sweep_index in range(COARSE_SWEEPS - 1):
        padded = pad_coarse(correction)
        padded_z = jnp.pad(correction, ((0, 0), (0, 0), (1, 1)))
        offdiag = stacked[2] * padded[:-2, 1:-1] + stacked[3] * padded[2:, 1:-1]
        offdiag = offdiag + stacked[4] * padded[1:-1, :-2] + stacked[5] * padded[1:-1, 2:]
        offdiag = offdiag + stacked[6] * padded_z[:, :, :-2] + stacked[7] * padded_z[:, :, 2:]
        correction = correction + RELAX_WEIGHT * (coarse_residual - coarse_diag * correction + offdiag) / coarse_diag
    return correction

def prolong(correction):
    dims = correction.shape
    wide = jnp.broadcast_to(correction[:, None, :, None, :, None], (dims[0], COARSEN, dims[1], COARSEN, dims[2], COARSEN))
    return wide.reshape(dims[0] * COARSEN, dims[1] * COARSEN, dims[2] * COARSEN)

def pad_plane(values):
    return jnp.pad(values, ((1, 1), (1, 1), (0, 0)))

def reference(right_side, knudsen, solid):
    pore_mask = (1 - solid).astype(jnp.float32)
    root_coef = jnp.sqrt(knudsen * pore_mask)
    source = right_side * pore_mask
    coef_pad = pad_plane(root_coef)
    diagonal = pore_mask * (MASS_TERM + root_coef * neighbours(coef_pad)) + (1.0 - pore_mask)
    inv_diag = 1.0 / diagonal
    scaled = source * inv_diag

    def coupling(iterate):
        return root_coef * neighbours(pad_plane(root_coef * iterate))
    iterate = RELAX_WEIGHT * scaled
    for sweep_index in range(PRE_SWEEPS - 1):
        iterate = iterate + RELAX_WEIGHT * (scaled - iterate + inv_diag * coupling(iterate))
    residual = source - diagonal * iterate + coupling(iterate)
    stacked = coarse_operator(coef_pad, pore_mask, residual)
    correction = coarse_relax(stacked, pad_plane)
    iterate = iterate + pore_mask * prolong(correction)
    for sweep_index in range(POST_SWEEPS):
        iterate = iterate + RELAX_WEIGHT * (scaled - iterate + inv_diag * coupling(iterate))
    return iterate
```

```python
import functools

import jax
import jax.numpy as jnp
from jax import lax
from jax.experimental import pallas as pl
from jax.experimental.pallas import tpu as pltpu
from jax.sharding import PartitionSpec as P

MESH = pl.DeviceIdType.MESH
F32 = jnp.float32
NREG, NBLK = 32, 8
XL = 24
YV = 9
XO = 3
MASS = 0.05
RELAX = 0.8

NEAR = [(dr, db) for dr in (-2, -1, 0, 1, 2) for db in (-1, 0, 1) if (dr, db) != (0, 0)]
FAR = [(dr, db) for dr in (-3, 3) for db in (-1, 0, 1)]
CORNERS = [(dr, db) for dr in (-1, 1) for db in (-1, 1)]


def iota(axis, shape=(8, 128)):
    return lax.broadcasted_iota(jnp.int32, shape, axis)


def z_sides(a, b):
    lane = iota(2, (1, 8, 128))
    first, last = lane == 0, lane == 127
    ra, rb = pltpu.roll(a, 1, 2), pltpu.roll(b, 1, 2)
    la, lb = pltpu.roll(a, 127, 2), pltpu.roll(b, 127, 2)
    low = (jnp.where(first, 0.0, ra), jnp.where(first, ra, rb))
    high = (jnp.where(last, lb, la), jnp.where(last, 0.0, lb))
    return low, high


def y_sides(a):
    down = jnp.concatenate([pltpu.roll(a[YV - 1 :], 1, 1), a[: YV - 1]], axis=0)
    up = jnp.concatenate([a[1:], pltpu.roll(a[:1], 7, 1)], axis=0)
    return down, up


def around(ref, X):
    a, b = ref[X, 0], ref[X, 1]
    low, high = z_sides(a, b)
    out = []
    for h, v in ((0, a), (1, b)):
        down, up = y_sides(v)
        out.append((low[h] + high[h]) + (down + up) + (ref[X - 1, h] + ref[X + 1, h]))
    return (a, b), out


def y_total(v):
    sub = iota(0)
    same, less, more = None, None, None
    for i in range(YV):
        lo, hi = 4 - i, 12 - i
        s = v[i]
        if i < 4:
            t = jnp.where((sub < lo) & (sub > 0), s, 0.0)
            less = t if less is None else less + t
            s = jnp.where(sub >= lo, s, 0.0)
        elif i > 4:
            t = jnp.where((sub >= hi) & (sub < 7), s, 0.0)
            more = t if more is None else more + t
            s = jnp.where(sub < hi, s, 0.0)
        same = s if same is None else same + s
    return same + pltpu.roll(less, 7, 0) + pltpu.roll(more, 1, 0)


def dot(a, b):
    return jnp.dot(a, b, precision=lax.Precision.HIGHEST, preferred_element_type=F32)


def kernel(
    k_ref, solid_ref, rs_ref, out_ref,
    kn, sn, cn, rn, cs, S, G, W, RC, UA, UB, on,
    ysend, yrecv, csend, crecv, usend, urecv, vsend, vrecv, xhalo,
    racc, tacc, cnt, czacc, cyacc, zacc, CM, RM, CO, RO, pz, px, po,
    load_sem, out_sem, ss, rr,
):
    r = lax.axis_index("region")
    b = lax.axis_index("block")

    def dev(dr, db):
        return (lax.rem(r + (dr + NREG), NREG), lax.rem(b + (db + NBLK), NBLK))

    bar = pltpu.get_barrier_semaphore()
    for off in NEAR + FAR:
        pl.semaphore_signal(bar, inc=1, device_id=dev(*off), device_id_type=MESH)

    loads = []
    for i, (src, dst) in enumerate(((k_ref, kn), (solid_ref, sn), (rs_ref, rn.at[2 : 2 + XL, :, 8:72, :]))):
        for h in range(2):
            cp = pltpu.make_async_copy(
                src.at[:, :, pl.ds(128 * h, 128)], dst.at[:, h], load_sem.at[2 * i + h]
            )
            cp.start()
            loads.append(cp)

    row, col = iota(0, (256, 128)), iota(1, (256, 128))
    cell = lax.rem(col, 32)
    pz[...] = jnp.where(lax.div(row, 8) == cell, 1.0, 0.0)
    po[...] = jnp.where(row == 8 * cell, 1.0, 0.0)
    row, col = iota(0, (128, 256)), iota(1, (128, 256))
    px[...] = jnp.where(row - 32 == lax.div(col, 8), 1.0, 0.0)
    zero8 = jnp.zeros((8, 128), F32)
    zeros9 = jnp.zeros((YV, 8, 128), F32)

    def clear(x, _):
        for h in range(2):
            cn[x, h, 0:8, :] = zero8
            cn[x, h, 72:80, :] = zero8
            rn[jnp.minimum(x, XL + 3), h, 0:8, :] = zero8
            rn[jnp.minimum(x, XL + 3), h, 72:80, :] = zero8
        return 0

    lax.fori_loop(0, XL + 2 * XO, clear, 0)
    for h in range(2):
        UB[XO - 1, h] = zeros9
        UB[XO + XL, h] = zeros9
        for s in range(3):
            for ref in (racc, cnt, czacc, cyacc):
                ref[s, h] = zeros9
            for ref in (tacc, zacc):
                ref[s, h] = zero8

    for cp in loads[:4]:
        cp.wait()

    def root(x, _):
        for h in range(2):
            k = kn[x, h]
            cn[x + XO, h, 8:72, :] = jnp.where(sn[x, h] == 0, k * lax.rsqrt(k), 0.0)
        return 0

    lax.fori_loop(0, XL, root, 0)
    for cp in loads[4:]:
        cp.wait()

    def pack(x, _):
        for h in range(2):
            for side in range(2):
                for j in range(3):
                    y = j if side == 0 else 61 + j
                    ysend[side, (x * 2 + h) * 3 + j] = cn[x + XO, h, 8 + y : 9 + y, :]
                for j in range(2):
                    y = j if side == 0 else 62 + j
                    ysend[side, 144 + (x * 2 + h) * 2 + j] = rn[x + 2, h, 8 + y : 9 + y, :]
        return 0

    lax.fori_loop(0, XL, pack, 0)
    for n, (dr, db) in enumerate(CORNERS):
        for p in range(2):
            x = p if dr < 0 else XL - 2 + p
            for h in range(2):
                for j in range(2):
                    y = j if db < 0 else 62 + j
                    csend[n, (p * 2 + h) * 2 + j] = cn[x + XO, h, 8 + y : 9 + y, :]
        x, y = 0 if dr < 0 else XL - 1, 0 if db < 0 else 63
        for h in range(2):
            csend[n, 8 + h] = rn[x + 2, h, 8 + y : 9 + y, :]

    pl.semaphore_wait(bar, len(NEAR) + len(FAR))

    count = [0]

    def remote(src, dst, off):
        n = count[0]
        count[0] += 1
        cp = pltpu.make_async_remote_copy(
            src_ref=src, dst_ref=dst, send_sem=ss.at[n], recv_sem=rr.at[n],
            device_id=dev(*off), device_id_type=MESH,
        )
        cp.start()
        return cp

    ymsg = [remote(ysend.at[0], yrecv.at[1], (0, -1)), remote(ysend.at[1], yrecv.at[0], (0, 1))]
    xmsg = [
        remote(cn.at[3:6, :, 8:72, :], cn.at[27:30, :, 8:72, :], (-1, 0)),
        remote(cn.at[24:27, :, 8:72, :], cn.at[0:3, :, 8:72, :], (1, 0)),
        remote(rn.at[2:4, :, 8:72, :], rn.at[26:28, :, 8:72, :], (-1, 0)),
        remote(rn.at[24:26, :, 8:72, :], rn.at[0:2, :, 8:72, :], (1, 0)),
    ]
    cmsg = [remote(csend.at[n], crecv.at[3 - n], off) for n, off in enumerate(CORNERS)]

    def strided(ref, X, h):
        return jnp.stack([ref[X, h, pl.ds(4 + i, 8, stride=9), :] for i in range(YV)], axis=0)

    def deal(x, _):
        X = x + XO
        c = [strided(cn, X, h) for h in range(2)]
        low, _high = z_sides(*c)
        slab = lax.div(x, 8)
        for h in range(2):
            cs[X, h] = c[h]
            cnt[slab, h] += jnp.where(c[h] > 0.0, 1.0, 0.0)
            czacc[slab, h] += c[h] * low[h]
            cyacc[slab, h] += c[h] * y_sides(c[h])[0]
        return 0

    lax.fori_loop(0, XL, deal, 0)

    for cp in ymsg:
        cp.wait()
    below = jnp.where(b > 0, 1.0, 0.0).astype(F32)
    above = jnp.where(b < NBLK - 1, 1.0, 0.0).astype(F32)
    left = jnp.where(r > 0, 1.0, 0.0).astype(F32)
    right = jnp.where(r < NREG - 1, 1.0, 0.0).astype(F32)

    def unpack(x, _):
        for h in range(2):
            at = (x * 2 + h) * 3
            for j in range(3):
                cs[x + XO, h, 1 + j, 0:1, :] = yrecv[0, at + j] * below
                cs[x + XO, h, 5 + j, 7:8, :] = yrecv[1, at + j] * above
            at = 144 + (x * 2 + h) * 2
            for j in range(2):
                rn[x + 2, h, 6 + j : 7 + j, :] = yrecv[0, at + j]
                rn[x + 2, h, 72 + j : 73 + j, :] = yrecv[1, at + j]
        return 0

    lax.fori_loop(0, XL, unpack, 0)
    sub = iota(0)

    def edge(v):
        return jnp.where(sub == 0, v[3], jnp.where(sub == 7, v[5], 0.0))

    def setup(X, own):
        c, near = around(cs, X)
        for h in range(2):
            d = MASS + c[h] * near[h]
            pore = c[h] > 0.0
            safe = jnp.where(pore, c[h], 1.0)
            both = 1.0 / (d * safe)
            g = RELAX * c[h] * (both * safe)
            G[X, h] = g * c[h]
            S[X, h] = g * strided(rn, X - 1, h)
            if own:
                rc = jnp.where(pore, both * d, 0.0)
                RC[X, h] = rc
                W[X, h] = (1.0 / RELAX) * d * rc
                zacc[lax.div(X - XO, 8), h] += edge(c[h]) * c[h][4]

    def sweep(src, X):
        u, near = around(src, X)
        return [0.2 * u[h] + (S[X, h] + G[X, h] * near[h]) for h in range(2)]

    def first(X):
        for h, v in enumerate(sweep(S, X)):
            UA[X, h] = v

    vec, subs = iota(0, (YV, 8, 128)), iota(1, (YV, 8, 128))
    place = subs * YV + vec
    inside = (place >= 4) & (place < 68)

    def second(X):
        for h, v in enumerate(sweep(UA, X)):
            UB[X, h] = jnp.where(inside, v, 0.0)

    def resid(X):
        u, near = around(UB, X)
        slab = lax.div(X - XO, 8)
        for h in range(2):
            racc[slab, h] += W[X, h] * (S[X, h] - RELAX * u[h] + G[X, h] * near[h])
            tacc[slab, h] += edge(cs[X, h]) * u[h][4]

    def run(fn, lo, hi):
        def body(X, _):
            fn(X)
            return 0

        lax.fori_loop(lo + XO, hi + XO, body, 0)

    own_setup = functools.partial(setup, own=True)
    halo_setup = functools.partial(setup, own=False)
    run(own_setup, 1, 23)
    run(first, 2, 22)
    run(second, 3, 21)
    run(resid, 4, 20)

    for cp in xmsg + cmsg:
        cp.wait()
    for X, side in ((0, left), (1, left), (2, left), (27, right), (28, right), (29, right)):
        for h in range(2):
            cs[X, h] = strided(cn, X, h) * side
    for n, (dr, db) in enumerate(CORNERS):
        side = (left if dr < 0 else right) * (below if db < 0 else above)
        for p in range(2):
            X = (1 + p) if dr < 0 else (27 + p)
            for h in range(2):
                for j in range(2):
                    v = crecv[n, (p * 2 + h) * 2 + j] * side
                    if db < 0:
                        cs[X, h, 2 + j, 0:1, :] = v
                    else:
                        cs[X, h, 5 + j, 7:8, :] = v
        X, y = (1 if dr < 0 else 26), (7 if db < 0 else 72)
        for h in range(2):
            rn[X, h, y : y + 1, :] = crecv[n, 8 + h]
    run(halo_setup, -2, 0)
    run(own_setup, 0, 1)
    run(own_setup, 23, 24)
    run(halo_setup, 24, 26)
    run(first, -1, 2)
    run(first, 22, 25)
    run(second, 0, 3)
    run(second, 21, 24)
    run(resid, 0, 4)
    run(resid, 20, 24)

    def halves(fn):
        return jnp.concatenate([fn(0), fn(1)], axis=1)

    parts = [halves(lambda h, s=s: y_total(racc[s, h])) for s in range(3)]
    parts += [halves(lambda h, s=s: tacc[s, h]) for s in range(3)]
    parts += [halves(lambda h: y_total(cs[2, h] * UB[3, h])), halves(lambda h: y_total(cs[27, h] * UB[26, h]))]
    tot = dot(jnp.concatenate(parts, axis=0), pz[...])
    tot = [tot[8 * i : 8 * i + 8] for i in range(8)]
    group = lax.div(iota(1), 32)
    faces = [tot[6], zero8, tot[7]]
    for s in range(3):
        RM[7 + s, 1] = jnp.where(
            group == 0, tot[s], jnp.where(group == 1, tot[3 + s], jnp.where(group == 2, faces[s], 0.0))
        )
    rmsg = [
        remote(RM.at[7:10, 1], RM.at[7 - 3 * dr : 10 - 3 * dr, 1 - db], (dr, db)) for dr, db in NEAR
    ]
    for dr, db in FAR:
        s, t = (9, 0) if dr > 0 else (7, 16)
        rmsg.append(remote(RM.at[s, 1], RM.at[t, 1 - db], (dr, db)))

    planes = [y_pair(cs, 2, 3), y_pair(cs, 10, 11), y_pair(cs, 18, 19), y_pair(cs, 26, 27)]
    parts = [halves(lambda h, s=s: y_total(cnt[s, h])) for s in range(3)]
    parts += [halves(lambda h, p=p: p[h]) for p in planes]
    turn = lax.rem(vec + subs, 8) == 4

    def y_face(s, h):
        return y_total(jnp.where(turn, cyacc[s, h], 0.0)) + jnp.where(sub == 0, zacc[s, h], 0.0)

    parts += [halves(lambda h, s=s: y_face(s, h)) for s in range(3)]
    parts += [halves(lambda h, s=s: zacc[s, h]) for s in range(3)]
    tot = dot(jnp.concatenate(parts, axis=0), pz[...])
    tot = [tot[8 * i : 8 * i + 8] for i in range(13)]
    tz = dot(jnp.concatenate([halves(lambda h, s=s: y_total(czacc[s, h])) for s in range(3)], axis=0), po[...])
    for s in range(3):
        cx, cx2, cy, cz = tot[3 + s], tot[4 + s], tot[7 + s], tz[8 * s : 8 * s + 8]
        cy2 = jnp.where(sub == 7, tot[10 + s], pltpu.roll(cy, 7, 0))
        diag = MASS * (tot[s] + 1.0) + cx + cx2 + cy + cy2 + cz + pltpu.roll(cz, 127, 1)
        CM[6 + s, 1] = jnp.where(
            group == 0, RELAX / diag, jnp.where(group == 1, cx, jnp.where(group == 2, cy, cz))
        )
    kmsg = [
        remote(CM.at[6:9, 1], CM.at[6 - 3 * dr : 9 - 3 * dr, 1 - db], (dr, db)) for dr, db in NEAR
    ]

    def upack(x, _):
        for h in range(2):
            for j in range(3):
                usend[0, (x * 2 + h) * 3 + j] = UB[x + XO, h, 4 + j, 0:1, :]
                usend[1, (x * 2 + h) * 3 + j] = UB[x + XO, h, 2 + j, 7:8, :]
        return 0

    lax.fori_loop(0, XL, upack, 0)
    for n, (dr, db) in enumerate(CORNERS):
        for p in range(2):
            X = XO + (p if dr < 0 else XL - 2 + p)
            for h in range(2):
                for j in range(2):
                    at = (p * 2 + h) * 2 + j
                    vsend[n, at] = UB[X, h, 4 + j, 0:1, :] if db < 0 else UB[X, h, 3 + j, 7:8, :]
    uymsg = [remote(usend.at[0], urecv.at[1], (0, -1)), remote(usend.at[1], urecv.at[0], (0, 1))]
    uxmsg = [remote(UB.at[3:6], xhalo.at[1], (-1, 0)), remote(UB.at[24:27], xhalo.at[0], (1, 0))]
    ucmsg = [remote(vsend.at[n], vrecv.at[3 - n], off) for n, off in enumerate(CORNERS)]

    def gather(msgs, g):
        out = jnp.where(group == 2, pltpu.roll(msgs[2], (2 - g) % 4 * 32, 1) if g != 2 else msgs[2], 0.0)
        out = jnp.where(group == 1, pltpu.roll(msgs[1], (1 - g) % 4 * 32, 1) if g != 1 else msgs[1], out)
        return jnp.where(group == 0, pltpu.roll(msgs[0], (-g) % 4 * 32, 1) if g != 0 else msgs[0], out)

    def down_y(v):
        t = pltpu.roll(v, 1, 0)
        return jnp.where(sub == 0, pltpu.roll(t, 32, 1), t)

    def up_y(v):
        t = pltpu.roll(v, 7, 0)
        return jnp.where(sub == 7, pltpu.roll(t, 96, 1), t)

    for cp in kmsg:
        cp.wait()

    def coarse(s, _):
        msgs = [CM[s, i] for i in range(3)]
        q = gather(msgs, 0)
        cx = gather(msgs, 1)
        cy = gather(msgs, 2)
        cz = gather(msgs, 3)
        after = gather([CM[jnp.minimum(s + 1, 14), i] for i in range(3)], 1)
        CO[s, 0] = q
        CO[s, 1] = q * cx
        CO[s, 2] = q * after
        CO[s, 3] = q * cy
        CO[s, 4] = q * up_y(cy)
        CO[s, 5] = q * cz
        CO[s, 6] = q * jnp.where(group < 3, pltpu.roll(cz, 127, 1), 0.0)
        return 0

    lax.fori_loop(0, 15, coarse, 0)

    for cp in uymsg + uxmsg + ucmsg:
        cp.wait()

    def uunpack(x, _):
        for h in range(2):
            for j in range(3):
                UB[x + XO, h, 1 + j, 0:1, :] = urecv[0, (x * 2 + h) * 3 + j] * below
                UB[x + XO, h, 5 + j, 7:8, :] = urecv[1, (x * 2 + h) * 3 + j] * above
        return 0

    lax.fori_loop(0, XL, uunpack, 0)
    for X, n, i, side in (
        (0, 0, 0, left), (1, 0, 1, left), (2, 0, 2, left),
        (27, 1, 0, right), (28, 1, 1, right), (29, 1, 2, right),
    ):
        for h in range(2):
            UB[X, h] = xhalo[n, i, h] * side
    for n, (dr, db) in enumerate(CORNERS):
        side = (left if dr < 0 else right) * (below if db < 0 else above)
        for p in range(2):
            X = (1 + p) if dr < 0 else (27 + p)
            for h in range(2):
                for j in range(2):
                    v = vrecv[n, (p * 2 + h) * 2 + j] * side
                    if db < 0:
                        UB[X, h, 2 + j, 0:1, :] = v
                    else:
                        UB[X, h, 5 + j, 7:8, :] = v

    for cp in rmsg:
        cp.wait()

    def rhs(s):
        msgs = [RM[s + 1, i] for i in range(3)]
        res = gather(msgs, 0)
        res = res + jnp.where(sub == 0, down_y(gather(msgs, 1)), jnp.where(sub == 7, up_y(gather(msgs, 1)), 0.0))
        if s % 3 == 0:
            res = res + gather([RM[s, i] for i in range(3)], 2)
        if s % 3 == 2:
            res = res + gather([RM[s + 2, i] for i in range(3)], 2)
        return res

    start = []
    for s in range(15):
        v = CO[s, 0] * rhs(s)
        RO[s] = v
        start.append(v)
    e = dict(enumerate(start))
    for it in range(1, 6):
        new = {}
        for s in range(it, 15 - it):
            v = e[s]
            off = CO[s, 1] * e[s - 1] + CO[s, 2] * e[s + 1]
            off = off + CO[s, 3] * down_y(v) + CO[s, 4] * up_y(v)
            off = off + CO[s, 5] * pltpu.roll(v, 1, 1) + CO[s, 6] * pltpu.roll(v, 127, 1)
            new[s] = 0.2 * v + (RO[s] + off)
        e = new
    parts = []
    for s in range(5, 10):
        parts += [e[s], down_y(e[s]), up_y(e[s])]
    wide = dot(jnp.concatenate(parts, axis=0), px[...])

    for s in range(5):
        for h in range(2):
            mid, dn, up = (wide[24 * s + 8 * i : 24 * s + 8 * i + 8, 128 * h : 128 * h + 128] for i in range(3))
            lay = []
            for i in range(YV):
                v = mid
                if i < 4:
                    v = jnp.where(sub < 4 - i, dn, v)
                elif i > 4:
                    v = jnp.where(sub >= 12 - i, up, v)
                lay.append(v)
            lay = jnp.stack(lay, axis=0)
            lo, hi = ((0, 3), (3, 11), (11, 19), (19, 27), (27, 30))[s]

            def add(X, _, lay=lay, h=h):
                UA[X, h] = UB[X, h] + cs[X, h] * lay
                return 0

            lax.fori_loop(lo, hi, add, 0)

    def third(X):
        for h, v in enumerate(sweep(UA, X)):
            UB[X, h] = v

    def fourth(X):
        for h, v in enumerate(sweep(UB, X)):
            UA[X, h] = v

    def fifth(X):
        for h, v in enumerate(sweep(UA, X)):
            v = v * RC[X, h]
            for i in range(YV):
                on[X - XO, h, pl.ds(4 + i, 8, stride=9), :] = v[i]

    run(third, -2, 26)
    run(fourth, -1, 25)
    outs = []
    for n in range(4):
        run(fifth, 6 * n, 6 * n + 6)
        for h in range(2):
            cp = pltpu.make_async_copy(
                on.at[6 * n : 6 * n + 6, h, 8:72, :],
                out_ref.at[6 * n : 6 * n + 6, :, pl.ds(128 * h, 128)],
                out_sem.at[2 * n + h],
            )
            cp.start()
            outs.append(cp)
    for cp in outs:
        cp.wait()


def y_pair(ref, X, X2):
    return [y_total(ref[X, h] * ref[X2, h]) for h in range(2)]


def vmem(*shape):
    return pltpu.VMEM(shape, F32)


def shards(right_side, knudsen, solid):
    n_msg = 10 + 20 + 14 + 8
    scratch = [
        vmem(XL, 2, 64, 128), pltpu.VMEM((XL, 2, 64, 128), jnp.int32), vmem(30, 2, 80, 128), vmem(28, 2, 80, 128),
    ]
    scratch += [vmem(30, 2, YV, 8, 128) for _ in range(7)]
    scratch += [vmem(XL, 2, 80, 128)]
    scratch += [vmem(2, 240, 1, 128), vmem(2, 240, 1, 128), vmem(4, 10, 1, 128), vmem(4, 10, 1, 128)]
    scratch += [vmem(2, 144, 1, 128), vmem(2, 144, 1, 128), vmem(4, 8, 1, 128), vmem(4, 8, 1, 128)]
    scratch += [vmem(2, 3, 2, YV, 8, 128)]
    scratch += [
        vmem(3, 2, YV, 8, 128), vmem(3, 2, 8, 128), vmem(3, 2, YV, 8, 128), vmem(3, 2, YV, 8, 128),
        vmem(3, 2, YV, 8, 128), vmem(3, 2, 8, 128),
    ]
    scratch += [vmem(15, 3, 8, 128), vmem(17, 3, 8, 128), vmem(15, 7, 8, 128), vmem(15, 8, 128)]
    scratch += [vmem(256, 128), vmem(128, 256), vmem(256, 128)]
    scratch += [
        pltpu.SemaphoreType.DMA((6,)), pltpu.SemaphoreType.DMA((8,)),
        pltpu.SemaphoreType.DMA((n_msg,)), pltpu.SemaphoreType.DMA((n_msg,)),
    ]
    return pl.pallas_call(
        kernel,
        name="vcycle",
        out_shape=jax.ShapeDtypeStruct(right_side.shape, F32),
        in_specs=[pl.BlockSpec(memory_space=pl.ANY)] * 3,
        out_specs=pl.BlockSpec(memory_space=pl.ANY),
        scratch_shapes=scratch,
        compiler_params=pltpu.CompilerParams(
            collective_id=0, has_side_effects=True, vmem_limit_bytes=60 * 2**20
        ),
    )(knudsen, solid, right_side)


def solution(mesh):
    placed = P("region", "block", None)
    return jax.shard_map(shards, mesh=mesh, in_specs=(placed,) * 3, out_specs=placed, check_vma=False)
```

```python
import functools

import jax
import jax.numpy as jnp
from jax import lax
from jax.experimental import pallas as pl
from jax.experimental.pallas import tpu as pltpu
from jax.sharding import PartitionSpec as P

MESH = pl.DeviceIdType.MESH
F32 = jnp.float32
NREG, NBLK = 32, 8
XL = 24
YV = 9
XO = 3
MASS = 0.05
RELAX = 0.8

NEAR = [(dr, db) for dr in (-2, -1, 0, 1, 2) for db in (-1, 0, 1) if (dr, db) != (0, 0)]
FAR = [(dr, db) for dr in (-3, 3) for db in (-1, 0, 1)]
CORNERS = [(dr, db) for dr in (-1, 1) for db in (-1, 1)]


def iota(axis, shape=(8, 128)):
    return lax.broadcasted_iota(jnp.int32, shape, axis)


def z_sides(a, b):
    lane = iota(2, (1, 8, 128))
    first, last = lane == 0, lane == 127
    ra, rb = pltpu.roll(a, 1, 2), pltpu.roll(b, 1, 2)
    la, lb = pltpu.roll(a, 127, 2), pltpu.roll(b, 127, 2)
    low = (jnp.where(first, 0.0, ra), jnp.where(first, ra, rb))
    high = (jnp.where(last, lb, la), jnp.where(last, 0.0, lb))
    return low, high


def y_sides(a):
    down = jnp.concatenate([pltpu.roll(a[YV - 1 :], 1, 1), a[: YV - 1]], axis=0)
    up = jnp.concatenate([a[1:], pltpu.roll(a[:1], 7, 1)], axis=0)
    return down, up


def around(ref, X):
    a, b = ref[X, 0], ref[X, 1]
    low, high = z_sides(a, b)
    out = []
    for h, v in ((0, a), (1, b)):
        down, up = y_sides(v)
        out.append((low[h] + high[h]) + (down + up) + (ref[X - 1, h] + ref[X + 1, h]))
    return (a, b), out


def y_total(v):
    sub = iota(0)
    same, less, more = None, None, None
    for i in range(YV):
        lo, hi = 4 - i, 12 - i
        s = v[i]
        if i < 4:
            t = jnp.where((sub < lo) & (sub > 0), s, 0.0)
            less = t if less is None else less + t
            s = jnp.where(sub >= lo, s, 0.0)
        elif i > 4:
            t = jnp.where((sub >= hi) & (sub < 7), s, 0.0)
            more = t if more is None else more + t
            s = jnp.where(sub < hi, s, 0.0)
        same = s if same is None else same + s
    return same + pltpu.roll(less, 7, 0) + pltpu.roll(more, 1, 0)


def dot(a, b):
    return jnp.dot(a, b, precision=lax.Precision.HIGHEST, preferred_element_type=F32)


def kernel(
    k_ref, solid_ref, rs_ref, out_ref,
    kn, sn, cn, rn, cs, S, G, W, RC, UA, UB, on,
    ysend, yrecv, csend, crecv, usend, urecv, vsend, vrecv, xhalo,
    racc, tacc, cnt, czacc, cyacc, zacc, CM, RM, CO, RO, pz, px, po,
    load_sem, out_sem, ss, rr,
):
    r = lax.axis_index("region")
    b = lax.axis_index("block")

    def dev(dr, db):
        return (lax.rem(r + (dr + NREG), NREG), lax.rem(b + (db + NBLK), NBLK))

    bar = pltpu.get_barrier_semaphore()
    for off in NEAR + FAR:
        pl.semaphore_signal(bar, inc=1, device_id=dev(*off), device_id_type=MESH)

    loads = []
    for i, (src, dst) in enumerate(((k_ref, kn), (solid_ref, sn), (rs_ref, rn.at[2 : 2 + XL, :, 8:72, :]))):
        for h in range(2):
            cp = pltpu.make_async_copy(
                src.at[:, :, pl.ds(128 * h, 128)], dst.at[:, h], load_sem.at[2 * i + h]
            )
            cp.start()
            loads.append(cp)

    row, col = iota(0, (256, 128)), iota(1, (256, 128))
    cell = lax.rem(col, 32)
    pz[...] = jnp.where(lax.div(row, 8) == cell, 1.0, 0.0)
    po[...] = jnp.where(row == 8 * cell, 1.0, 0.0)
    row, col = iota(0, (128, 256)), iota(1, (128, 256))
    px[...] = jnp.where(row - 32 == lax.div(col, 8), 1.0, 0.0)
    zero8 = jnp.zeros((8, 128), F32)
    zeros9 = jnp.zeros((YV, 8, 128), F32)

    def clear(x, _):
        for h in range(2):
            cn[x, h, 0:8, :] = zero8
            cn[x, h, 72:80, :] = zero8
            rn[jnp.minimum(x, XL + 3), h, 0:8, :] = zero8
            rn[jnp.minimum(x, XL + 3), h, 72:80, :] = zero8
        return 0

    lax.fori_loop(0, XL + 2 * XO, clear, 0)
    for h in range(2):
        UB[XO - 1, h] = zeros9
        UB[XO + XL, h] = zeros9
        for s in range(3):
            for ref in (racc, cnt, czacc, cyacc):
                ref[s, h] = zeros9
            for ref in (tacc, zacc):
                ref[s, h] = zero8

    for cp in loads[:4]:
        cp.wait()

    def root(x, _):
        for h in range(2):
            k = kn[x, h]
            cn[x + XO, h, 8:72, :] = jnp.where(sn[x, h] == 0, k * lax.rsqrt(k), 0.0)
        return 0

    lax.fori_loop(0, XL, root, 0, unroll=2)
    for cp in loads[4:]:
        cp.wait()

    def pack(x, _):
        for h in range(2):
            for side in range(2):
                for j in range(3):
                    y = j if side == 0 else 61 + j
                    ysend[side, (x * 2 + h) * 3 + j] = cn[x + XO, h, 8 + y : 9 + y, :]
                for j in range(2):
                    y = j if side == 0 else 62 + j
                    ysend[side, 144 + (x * 2 + h) * 2 + j] = rn[x + 2, h, 8 + y : 9 + y, :]
        return 0

    lax.fori_loop(0, XL, pack, 0)
    for n, (dr, db) in enumerate(CORNERS):
        for p in range(2):
            x = p if dr < 0 else XL - 2 + p
            for h in range(2):
                for j in range(2):
                    y = j if db < 0 else 62 + j
                    csend[n, (p * 2 + h) * 2 + j] = cn[x + XO, h, 8 + y : 9 + y, :]
        x, y = 0 if dr < 0 else XL - 1, 0 if db < 0 else 63
        for h in range(2):
            csend[n, 8 + h] = rn[x + 2, h, 8 + y : 9 + y, :]

    pl.semaphore_wait(bar, len(NEAR) + len(FAR))

    count = [0]

    def remote(src, dst, off):
        n = count[0]
        count[0] += 1
        cp = pltpu.make_async_remote_copy(
            src_ref=src, dst_ref=dst, send_sem=ss.at[n], recv_sem=rr.at[n],
            device_id=dev(*off), device_id_type=MESH,
        )
        cp.start()
        return cp

    ymsg = [remote(ysend.at[0], yrecv.at[1], (0, -1)), remote(ysend.at[1], yrecv.at[0], (0, 1))]
    xmsg = [
        remote(cn.at[3:6, :, 8:72, :], cn.at[27:30, :, 8:72, :], (-1, 0)),
        remote(cn.at[24:27, :, 8:72, :], cn.at[0:3, :, 8:72, :], (1, 0)),
        remote(rn.at[2:4, :, 8:72, :], rn.at[26:28, :, 8:72, :], (-1, 0)),
        remote(rn.at[24:26, :, 8:72, :], rn.at[0:2, :, 8:72, :], (1, 0)),
    ]
    cmsg = [remote(csend.at[n], crecv.at[3 - n], off) for n, off in enumerate(CORNERS)]

    def strided(ref, X, h):
        return jnp.stack([ref[X, h, pl.ds(4 + i, 8, stride=9), :] for i in range(YV)], axis=0)

    def deal(x, _):
        X = x + XO
        c = [strided(cn, X, h) for h in range(2)]
        low, _high = z_sides(*c)
        slab = lax.div(x, 8)
        for h in range(2):
            cs[X, h] = c[h]
            cnt[slab, h] += jnp.where(c[h] > 0.0, 1.0, 0.0)
            czacc[slab, h] += c[h] * low[h]
            cyacc[slab, h] += c[h] * y_sides(c[h])[0]
        return 0

    lax.fori_loop(0, XL, deal, 0, unroll=4)

    for cp in ymsg:
        cp.wait()
    below = jnp.where(b > 0, 1.0, 0.0).astype(F32)
    above = jnp.where(b < NBLK - 1, 1.0, 0.0).astype(F32)
    left = jnp.where(r > 0, 1.0, 0.0).astype(F32)
    right = jnp.where(r < NREG - 1, 1.0, 0.0).astype(F32)

    def unpack(x, _):
        for h in range(2):
            at = (x * 2 + h) * 3
            for j in range(3):
                cs[x + XO, h, 1 + j, 0:1, :] = yrecv[0, at + j] * below
                cs[x + XO, h, 5 + j, 7:8, :] = yrecv[1, at + j] * above
            at = 144 + (x * 2 + h) * 2
            for j in range(2):
                rn[x + 2, h, 6 + j : 7 + j, :] = yrecv[0, at + j]
                rn[x + 2, h, 72 + j : 73 + j, :] = yrecv[1, at + j]
        return 0

    lax.fori_loop(0, XL, unpack, 0)
    sub = iota(0)

    def edge(v):
        return jnp.where(sub == 0, v[3], jnp.where(sub == 7, v[5], 0.0))

    def setup(X, own):
        c, near = around(cs, X)
        for h in range(2):
            d = MASS + c[h] * near[h]
            pore = c[h] > 0.0
            safe = jnp.where(pore, c[h], 1.0)
            both = 1.0 / (d * safe)
            g = RELAX * c[h] * (both * safe)
            G[X, h] = g * c[h]
            S[X, h] = g * strided(rn, X - 1, h)
            if own:
                rc = jnp.where(pore, both * d, 0.0)
                RC[X, h] = rc
                W[X, h] = (1.0 / RELAX) * d * rc
                zacc[lax.div(X - XO, 8), h] += edge(c[h]) * c[h][4]

    def sweep(src, X):
        u, near = around(src, X)
        return [0.2 * u[h] + (S[X, h] + G[X, h] * near[h]) for h in range(2)]

    def first(X):
        for h, v in enumerate(sweep(S, X)):
            UA[X, h] = v

    vec, subs = iota(0, (YV, 8, 128)), iota(1, (YV, 8, 128))
    place = subs * YV + vec
    inside = (place >= 4) & (place < 68)

    def second(X):
        for h, v in enumerate(sweep(UA, X)):
            UB[X, h] = jnp.where(inside, v, 0.0)

    def resid(X):
        u, near = around(UB, X)
        slab = lax.div(X - XO, 8)
        for h in range(2):
            racc[slab, h] += W[X, h] * (S[X, h] - RELAX * u[h] + G[X, h] * near[h])
            tacc[slab, h] += edge(cs[X, h]) * u[h][4]

    def run(fn, lo, hi, step=8):
        whole = (hi - lo) // step

        def body(i, _):
            for j in range(step):
                fn(lo + XO + i * step + j)
            return 0

        if whole:
            lax.fori_loop(0, whole, body, 0)
        for x in range(lo + whole * step, hi):
            fn(x + XO)

    own_setup = functools.partial(setup, own=True)
    run(own_setup, 1, 23, 8)
    run(first, 2, 22, 7)
    run(second, 3, 21, 6)
    run(resid, 4, 20, 8)

    for cp in xmsg + cmsg:
        cp.wait()
    for X, side in ((0, left), (1, left), (2, left), (27, right), (28, right), (29, right)):
        for h in range(2):
            cs[X, h] = strided(cn, X, h) * side
    for n, (dr, db) in enumerate(CORNERS):
        side = (left if dr < 0 else right) * (below if db < 0 else above)
        for p in range(2):
            X = (1 + p) if dr < 0 else (27 + p)
            for h in range(2):
                for j in range(2):
                    v = crecv[n, (p * 2 + h) * 2 + j] * side
                    if db < 0:
                        cs[X, h, 2 + j, 0:1, :] = v
                    else:
                        cs[X, h, 5 + j, 7:8, :] = v
        X, y = (1 if dr < 0 else 26), (7 if db < 0 else 72)
        for h in range(2):
            rn[X, h, y : y + 1, :] = crecv[n, 8 + h]
    for x in (-2, -1, 0, 23, 24, 25):
        setup(x + XO, 0 <= x < XL)
    for x in (-1, 0, 1, 22, 23, 24):
        first(x + XO)
    for x in (0, 1, 2, 21, 22, 23):
        second(x + XO)
    for x in (0, 1, 2, 3, 20, 21, 22, 23):
        resid(x + XO)

    def halves(fn):
        return jnp.concatenate([fn(0), fn(1)], axis=1)

    parts = [halves(lambda h, s=s: y_total(racc[s, h])) for s in range(3)]
    parts += [halves(lambda h, s=s: tacc[s, h]) for s in range(3)]
    parts += [halves(lambda h: y_total(cs[2, h] * UB[3, h])), halves(lambda h: y_total(cs[27, h] * UB[26, h]))]
    tot = dot(jnp.concatenate(parts, axis=0), pz[...])
    tot = [tot[8 * i : 8 * i + 8] for i in range(8)]
    group = lax.div(iota(1), 32)
    faces = [tot[6], zero8, tot[7]]
    for s in range(3):
        RM[7 + s, 1] = jnp.where(
            group == 0, tot[s], jnp.where(group == 1, tot[3 + s], jnp.where(group == 2, faces[s], 0.0))
        )
    rmsg = [
        remote(RM.at[7:10, 1], RM.at[7 - 3 * dr : 10 - 3 * dr, 1 - db], (dr, db)) for dr, db in NEAR
    ]
    for dr, db in FAR:
        s, t = (9, 0) if dr > 0 else (7, 16)
        rmsg.append(remote(RM.at[s, 1], RM.at[t, 1 - db], (dr, db)))

    planes = [y_pair(cs, 2, 3), y_pair(cs, 10, 11), y_pair(cs, 18, 19), y_pair(cs, 26, 27)]
    parts = [halves(lambda h, s=s: y_total(cnt[s, h])) for s in range(3)]
    parts += [halves(lambda h, p=p: p[h]) for p in planes]
    turn = lax.rem(vec + subs, 8) == 4

    def y_face(s, h):
        return y_total(jnp.where(turn, cyacc[s, h], 0.0)) + jnp.where(sub == 0, zacc[s, h], 0.0)

    parts += [halves(lambda h, s=s: y_face(s, h)) for s in range(3)]
    parts += [halves(lambda h, s=s: zacc[s, h]) for s in range(3)]
    tot = dot(jnp.concatenate(parts, axis=0), pz[...])
    tot = [tot[8 * i : 8 * i + 8] for i in range(13)]
    tz = dot(jnp.concatenate([halves(lambda h, s=s: y_total(czacc[s, h])) for s in range(3)], axis=0), po[...])
    for s in range(3):
        cx, cx2, cy, cz = tot[3 + s], tot[4 + s], tot[7 + s], tz[8 * s : 8 * s + 8]
        cy2 = jnp.where(sub == 7, tot[10 + s], pltpu.roll(cy, 7, 0))
        diag = MASS * (tot[s] + 1.0) + cx + cx2 + cy + cy2 + cz + pltpu.roll(cz, 127, 1)
        CM[6 + s, 1] = jnp.where(
            group == 0, RELAX / diag, jnp.where(group == 1, cx, jnp.where(group == 2, cy, cz))
        )
    kmsg = [
        remote(CM.at[6:9, 1], CM.at[6 - 3 * dr : 9 - 3 * dr, 1 - db], (dr, db)) for dr, db in NEAR
    ]

    def upack(x, _):
        for h in range(2):
            for j in range(3):
                usend[0, (x * 2 + h) * 3 + j] = UB[x + XO, h, 4 + j, 0:1, :]
                usend[1, (x * 2 + h) * 3 + j] = UB[x + XO, h, 2 + j, 7:8, :]
        return 0

    lax.fori_loop(0, XL, upack, 0)
    for n, (dr, db) in enumerate(CORNERS):
        for p in range(2):
            X = XO + (p if dr < 0 else XL - 2 + p)
            for h in range(2):
                for j in range(2):
                    at = (p * 2 + h) * 2 + j
                    vsend[n, at] = UB[X, h, 4 + j, 0:1, :] if db < 0 else UB[X, h, 3 + j, 7:8, :]
    uymsg = [remote(usend.at[0], urecv.at[1], (0, -1)), remote(usend.at[1], urecv.at[0], (0, 1))]
    uxmsg = [remote(UB.at[3:6], xhalo.at[1], (-1, 0)), remote(UB.at[24:27], xhalo.at[0], (1, 0))]
    ucmsg = [remote(vsend.at[n], vrecv.at[3 - n], off) for n, off in enumerate(CORNERS)]

    def turned(v, groups):
        return pltpu.roll(v, groups % 4 * 32, v.ndim - 1) if groups % 4 else v

    def gather(msgs, g):
        out = jnp.where(group == 2, turned(msgs[2], 2 - g), 0.0)
        out = jnp.where(group == 1, turned(msgs[1], 1 - g), out)
        return jnp.where(group == 0, turned(msgs[0], -g), out)

    def down_y(v):
        t = pltpu.roll(v, 1, v.ndim - 2)
        return jnp.where(sub == 0, turned(t, 1), t)

    def up_y(v):
        t = pltpu.roll(v, 7, v.ndim - 2)
        return jnp.where(sub == 7, turned(t, -1), t)

    for cp in kmsg:
        cp.wait()

    msgs = [CM[:, i] for i in range(3)]
    q = gather(msgs, 0)
    cx = gather(msgs, 1)
    cy = gather(msgs, 2)
    cz = gather(msgs, 3)
    CO[:, 0] = q
    CO[:, 1] = q * cx
    CO[0:14, 2] = q[0:14] * cx[1:15]
    CO[:, 3] = q * cy
    CO[:, 4] = q * up_y(cy)
    CO[:, 5] = q * cz
    CO[:, 6] = q * jnp.where(group < 3, pltpu.roll(cz, 127, 2), 0.0)

    for cp in uymsg + uxmsg + ucmsg:
        cp.wait()

    def uunpack(x, _):
        for h in range(2):
            for j in range(3):
                UB[x + XO, h, 1 + j, 0:1, :] = urecv[0, (x * 2 + h) * 3 + j] * below
                UB[x + XO, h, 5 + j, 7:8, :] = urecv[1, (x * 2 + h) * 3 + j] * above
        return 0

    lax.fori_loop(0, XL, uunpack, 0)
    for X, n, i, side in (
        (0, 0, 0, left), (1, 0, 1, left), (2, 0, 2, left),
        (27, 1, 0, right), (28, 1, 1, right), (29, 1, 2, right),
    ):
        for h in range(2):
            UB[X, h] = xhalo[n, i, h] * side
    for n, (dr, db) in enumerate(CORNERS):
        side = (left if dr < 0 else right) * (below if db < 0 else above)
        for p in range(2):
            X = (1 + p) if dr < 0 else (27 + p)
            for h in range(2):
                for j in range(2):
                    v = vrecv[n, (p * 2 + h) * 2 + j] * side
                    if db < 0:
                        UB[X, h, 2 + j, 0:1, :] = v
                    else:
                        UB[X, h, 5 + j, 7:8, :] = v

    for cp in rmsg:
        cp.wait()

    msgs = [RM[:, i] for i in range(3)]
    res = gather([m[1:16] for m in msgs], 0)
    face = gather([m[1:16] for m in msgs], 1)
    res = res + jnp.where(sub == 0, down_y(face), jnp.where(sub == 7, up_y(face), 0.0))
    face = gather(msgs, 2)
    start = []
    for s in range(15):
        v = res[s]
        if s % 3 == 0:
            v = v + face[s]
        if s % 3 == 2:
            v = v + face[s + 2]
        v = CO[s, 0] * v
        RO[s] = v
        start.append(v)
    e = dict(enumerate(start))
    for it in range(1, 6):
        new = {}
        for s in range(it, 15 - it):
            v = e[s]
            off = CO[s, 1] * e[s - 1] + CO[s, 2] * e[s + 1]
            off = off + CO[s, 3] * down_y(v) + CO[s, 4] * up_y(v)
            off = off + CO[s, 5] * pltpu.roll(v, 1, 1) + CO[s, 6] * pltpu.roll(v, 127, 1)
            new[s] = 0.2 * v + (RO[s] + off)
        e = new
    parts = []
    for s in range(5, 10):
        parts += [e[s], down_y(e[s]), up_y(e[s])]
    wide = dot(jnp.concatenate(parts, axis=0), px[...])

    for s in range(5):
        for h in range(2):
            mid, dn, up = (wide[24 * s + 8 * i : 24 * s + 8 * i + 8, 128 * h : 128 * h + 128] for i in range(3))
            lay = []
            for i in range(YV):
                v = mid
                if i < 4:
                    v = jnp.where(sub < 4 - i, dn, v)
                elif i > 4:
                    v = jnp.where(sub >= 12 - i, up, v)
                lay.append(v)
            lay = jnp.stack(lay, axis=0)
            lo, hi = ((0, 3), (3, 11), (11, 19), (19, 27), (27, 30))[s]

            def add(X, _, lay=lay, h=h):
                UA[X, h] = UB[X, h] + cs[X, h] * lay
                return 0

            lax.fori_loop(lo, hi, add, 0)

    def third(X):
        for h, v in enumerate(sweep(UA, X)):
            UB[X, h] = v

    def fourth(X):
        for h, v in enumerate(sweep(UB, X)):
            UA[X, h] = v

    def fifth(X):
        for h, v in enumerate(sweep(UA, X)):
            v = v * RC[X, h]
            for i in range(YV):
                on[X - XO, h, pl.ds(4 + i, 8, stride=9), :] = v[i]

    run(third, -2, 26, 7)
    run(fourth, -1, 25, 13)
    outs = []
    for n in range(4):
        run(fifth, 6 * n, 6 * n + 6, 6)
        for h in range(2):
            cp = pltpu.make_async_copy(
                on.at[6 * n : 6 * n + 6, h, 8:72, :],
                out_ref.at[6 * n : 6 * n + 6, :, pl.ds(128 * h, 128)],
                out_sem.at[2 * n + h],
            )
            cp.start()
            outs.append(cp)
    for cp in outs:
        cp.wait()


def y_pair(ref, X, X2):
    return [y_total(ref[X, h] * ref[X2, h]) for h in range(2)]


def vmem(*shape):
    return pltpu.VMEM(shape, F32)


def shards(right_side, knudsen, solid):
    n_msg = 10 + 20 + 14 + 8
    scratch = [
        vmem(XL, 2, 64, 128), pltpu.VMEM((XL, 2, 64, 128), jnp.int32), vmem(30, 2, 80, 128), vmem(28, 2, 80, 128),
    ]
    scratch += [vmem(30, 2, YV, 8, 128) for _ in range(7)]
    scratch += [vmem(XL, 2, 80, 128)]
    scratch += [vmem(2, 240, 1, 128), vmem(2, 240, 1, 128), vmem(4, 10, 1, 128), vmem(4, 10, 1, 128)]
    scratch += [vmem(2, 144, 1, 128), vmem(2, 144, 1, 128), vmem(4, 8, 1, 128), vmem(4, 8, 1, 128)]
    scratch += [vmem(2, 3, 2, YV, 8, 128)]
    scratch += [
        vmem(3, 2, YV, 8, 128), vmem(3, 2, 8, 128), vmem(3, 2, YV, 8, 128), vmem(3, 2, YV, 8, 128),
        vmem(3, 2, YV, 8, 128), vmem(3, 2, 8, 128),
    ]
    scratch += [vmem(15, 3, 8, 128), vmem(17, 3, 8, 128), vmem(15, 7, 8, 128), vmem(15, 8, 128)]
    scratch += [vmem(256, 128), vmem(128, 256), vmem(256, 128)]
    scratch += [
        pltpu.SemaphoreType.DMA((6,)), pltpu.SemaphoreType.DMA((8,)),
        pltpu.SemaphoreType.DMA((n_msg,)), pltpu.SemaphoreType.DMA((n_msg,)),
    ]
    return pl.pallas_call(
        kernel,
        name="vcycle",
        out_shape=jax.ShapeDtypeStruct(right_side.shape, F32),
        in_specs=[pl.BlockSpec(memory_space=pl.ANY)] * 3,
        out_specs=pl.BlockSpec(memory_space=pl.ANY),
        scratch_shapes=scratch,
        compiler_params=pltpu.CompilerParams(
            collective_id=0, has_side_effects=True, vmem_limit_bytes=60 * 2**20
        ),
    )(knudsen, solid, right_side)


def solution(mesh):
    placed = P("region", "block", None)
    return jax.shard_map(shards, mesh=mesh, in_specs=(placed,) * 3, out_specs=placed, check_vma=False)
```

```python
import functools

import jax
import jax.numpy as jnp
from jax import lax
from jax.experimental import pallas as pl
from jax.experimental.pallas import tpu as pltpu
from jax.sharding import PartitionSpec as P

MESH = pl.DeviceIdType.MESH
F32 = jnp.float32
NREG, NBLK = 32, 8
XL = 24
YV = 9
XO = 3
NCH, CH = 4, 6
CROWS = CH * 6
MASS = 0.05
RELAX = 0.8

NEAR = [(dr, db) for dr in (-2, -1, 0, 1, 2) for db in (-1, 0, 1) if (dr, db) != (0, 0)]
FAR = [(dr, db) for dr in (-3, 3) for db in (-1, 0, 1)]
CORNERS = [(dr, db) for dr in (-1, 1) for db in (-1, 1)]


def iota(axis, shape=(8, 128)):
    return lax.broadcasted_iota(jnp.int32, shape, axis)


def z_sides(a, b):
    lane = iota(2, (1, 8, 128))
    first, last = lane == 0, lane == 127
    ra, rb = pltpu.roll(a, 1, 2), pltpu.roll(b, 1, 2)
    la, lb = pltpu.roll(a, 127, 2), pltpu.roll(b, 127, 2)
    low = (jnp.where(first, 0.0, ra), jnp.where(first, ra, rb))
    high = (jnp.where(last, lb, la), jnp.where(last, 0.0, lb))
    return low, high


def y_sides(a):
    down = jnp.concatenate([pltpu.roll(a[YV - 1 :], 1, 1), a[: YV - 1]], axis=0)
    up = jnp.concatenate([a[1:], pltpu.roll(a[:1], 7, 1)], axis=0)
    return down, up


def around(ref, X):
    a, b = ref[X, 0], ref[X, 1]
    low, high = z_sides(a, b)
    out = []
    for h, v in ((0, a), (1, b)):
        down, up = y_sides(v)
        out.append((low[h] + high[h]) + (down + up) + (ref[X - 1, h] + ref[X + 1, h]))
    return (a, b), out


def y_total(v):
    sub = iota(0)
    same, less, more = None, None, None
    for i in range(YV):
        lo, hi = 4 - i, 12 - i
        s = v[i]
        if i < 4:
            t = jnp.where((sub < lo) & (sub > 0), s, 0.0)
            less = t if less is None else less + t
            s = jnp.where(sub >= lo, s, 0.0)
        elif i > 4:
            t = jnp.where((sub >= hi) & (sub < 7), s, 0.0)
            more = t if more is None else more + t
            s = jnp.where(sub < hi, s, 0.0)
        same = s if same is None else same + s
    return same + pltpu.roll(less, 7, 0) + pltpu.roll(more, 1, 0)


def dot(a, b):
    return jnp.dot(a, b, precision=lax.Precision.HIGHEST, preferred_element_type=F32)


def kernel(
    k_ref, solid_ref, rs_ref, out_ref,
    kn, sn, cn, rn, cs, S, G, W, RC, UA, UB, on,
    ysend, yrecv, csend, crecv, usend, urecv, vsend, vrecv, xhalo,
    racc, tacc, cnt, czacc, cyacc, zacc, CM, RM, CO, RO, pz, px, po,
    rsn, EC, load_sem, out_sem, ss, rr,
):
    r = lax.axis_index("region")
    b = lax.axis_index("block")

    def dev(dr, db):
        return (lax.rem(r + (dr + NREG), NREG), lax.rem(b + (db + NBLK), NBLK))

    bar = pltpu.get_barrier_semaphore()
    for off in NEAR + FAR:
        pl.semaphore_signal(bar, inc=1, device_id=dev(*off), device_id_type=MESH)

    loads = []
    for n in range(NCH):
        part = pl.ds(n * CH, CH)
        for i, (src, dst) in enumerate(((k_ref, kn), (solid_ref, sn), (rs_ref, rsn))):
            cp = pltpu.make_async_copy(src.at[part], dst.at[part], load_sem.at[3 * n + i])
            cp.start()
            loads.append(cp)

    row, col = iota(0, (256, 128)), iota(1, (256, 128))
    cell = lax.rem(col, 32)
    pz[...] = jnp.where(lax.div(row, 8) == cell, 1.0, 0.0)
    po[...] = jnp.where(row == 8 * cell, 1.0, 0.0)
    row, col = iota(0, (128, 256)), iota(1, (128, 256))
    px[...] = jnp.where(row - 32 == lax.div(col, 8), 1.0, 0.0)
    zero8 = jnp.zeros((8, 128), F32)
    zeros9 = jnp.zeros((YV, 8, 128), F32)

    def clear(x, _):
        for h in range(2):
            cn[x, h, 0:8, :] = zero8
            cn[x, h, 72:80, :] = zero8
            rn[jnp.minimum(x, XL + 3), h, 0:8, :] = zero8
            rn[jnp.minimum(x, XL + 3), h, 72:80, :] = zero8
        return 0

    lax.fori_loop(0, XL + 2 * XO, clear, 0)
    for h in range(2):
        UB[XO - 1, h] = zeros9
        UB[XO + XL, h] = zeros9
        for s in range(3):
            for ref in (racc, cnt, czacc, cyacc):
                ref[s, h] = zeros9
            for ref in (tacc, zacc):
                ref[s, h] = zero8

    count = [0]

    def remote(src, dst, off):
        n = count[0]
        count[0] += 1
        cp = pltpu.make_async_remote_copy(
            src_ref=src, dst_ref=dst, send_sem=ss.at[n], recv_sem=rr.at[n],
            device_id=dev(*off), device_id_type=MESH,
        )
        cp.start()
        return cp

    ymsg = []
    for n in range(NCH):
        for cp in loads[3 * n : 3 * n + 3]:
            cp.wait()

        def root(i, _, n=n):
            x = n * CH + i
            for h in range(2):
                half = slice(128 * h, 128 * h + 128)
                k = kn[x, :, half]
                cn[x + XO, h, 8:72, :] = jnp.where(sn[x, :, half] == 0, k * lax.rsqrt(k), 0.0)
                rn[x + 2, h, 8:72, :] = rsn[x, :, half]
                for side in range(2):
                    for j in range(3):
                        y = j if side == 0 else 61 + j
                        ysend[side, n, (i * 2 + h) * 3 + j] = cn[x + XO, h, 8 + y : 9 + y, :]
                    for j in range(2):
                        y = j if side == 0 else 62 + j
                        ysend[side, n, CROWS + (i * 2 + h) * 2 + j] = rn[x + 2, h, 8 + y : 9 + y, :]
            return 0

        lax.fori_loop(0, CH, root, 0, unroll=2)
        if n == 0:
            pl.semaphore_wait(bar, len(NEAR) + len(FAR))
        ymsg.append([
            remote(ysend.at[0, n], yrecv.at[1, n], (0, -1)), remote(ysend.at[1, n], yrecv.at[0, n], (0, 1))
        ])

    for n, (dr, db) in enumerate(CORNERS):
        for p in range(2):
            x = p if dr < 0 else XL - 2 + p
            for h in range(2):
                for j in range(2):
                    y = j if db < 0 else 62 + j
                    csend[n, (p * 2 + h) * 2 + j] = cn[x + XO, h, 8 + y : 9 + y, :]
        x, y = 0 if dr < 0 else XL - 1, 0 if db < 0 else 63
        for h in range(2):
            csend[n, 8 + h] = rn[x + 2, h, 8 + y : 9 + y, :]
    xmsg = [
        remote(cn.at[3:6, :, 8:72, :], cn.at[27:30, :, 8:72, :], (-1, 0)),
        remote(cn.at[24:27, :, 8:72, :], cn.at[0:3, :, 8:72, :], (1, 0)),
        remote(rn.at[2:4, :, 8:72, :], rn.at[26:28, :, 8:72, :], (-1, 0)),
        remote(rn.at[24:26, :, 8:72, :], rn.at[0:2, :, 8:72, :], (1, 0)),
    ]
    cmsg = [remote(csend.at[n], crecv.at[3 - n], off) for n, off in enumerate(CORNERS)]

    def strided(ref, X, h):
        return jnp.stack([ref[X, h, pl.ds(4 + i, 8, stride=9), :] for i in range(YV)], axis=0)

    def deal(x, _):
        X = x + XO
        c = [strided(cn, X, h) for h in range(2)]
        low, _high = z_sides(*c)
        slab = lax.div(x, 8)
        for h in range(2):
            cs[X, h] = c[h]
            cnt[slab, h] += jnp.where(c[h] > 0.0, 1.0, 0.0)
            czacc[slab, h] += c[h] * low[h]
            cyacc[slab, h] += c[h] * y_sides(c[h])[0]
        return 0

    lax.fori_loop(0, XL, deal, 0, unroll=4)

    vec, subs = iota(0, (YV, 8, 128)), iota(1, (YV, 8, 128))
    place = subs * YV + vec
    inside = (place >= 4) & (place < 68)
    turn = lax.rem(vec + subs, 8) == 4

    def halves(fn):
        return jnp.concatenate([fn(0), fn(1)], axis=1)

    def faces(X):
        return halves(lambda h: y_total(cs[X, h] * cs[X + 1, h]))

    parts = [halves(lambda h, s=s: y_total(cnt[s, h])) for s in range(3)]
    parts += [halves(lambda h, s=s: y_total(jnp.where(turn, cyacc[s, h], 0.0))) for s in range(3)]
    parts += [faces(10), faces(18)]
    early = dot(jnp.concatenate(parts, axis=0), pz[...])
    for i in range(8):
        EC[i] = early[8 * i : 8 * i + 8]
    early = dot(jnp.concatenate([halves(lambda h, s=s: y_total(czacc[s, h])) for s in range(3)], axis=0), po[...])
    for i in range(3):
        EC[8 + i] = early[8 * i : 8 * i + 8]

    below = jnp.where(b > 0, 1.0, 0.0).astype(F32)
    above = jnp.where(b < NBLK - 1, 1.0, 0.0).astype(F32)
    left = jnp.where(r > 0, 1.0, 0.0).astype(F32)
    right = jnp.where(r < NREG - 1, 1.0, 0.0).astype(F32)

    def unpack(n):
        def body(i, _):
            x = n * CH + i
            for h in range(2):
                at = (i * 2 + h) * 3
                for j in range(3):
                    cs[x + XO, h, 1 + j, 0:1, :] = yrecv[0, n, at + j] * below
                    cs[x + XO, h, 5 + j, 7:8, :] = yrecv[1, n, at + j] * above
                at = CROWS + (i * 2 + h) * 2
                for j in range(2):
                    rn[x + 2, h, 6 + j : 7 + j, :] = yrecv[0, n, at + j]
                    rn[x + 2, h, 72 + j : 73 + j, :] = yrecv[1, n, at + j]
            return 0

        lax.fori_loop(0, CH, body, 0, unroll=2)

    sub = iota(0)

    def edge(v):
        return jnp.where(sub == 0, v[3], jnp.where(sub == 7, v[5], 0.0))

    def setup(X, own):
        c, near = around(cs, X)
        for h in range(2):
            d = MASS + c[h] * near[h]
            pore = c[h] > 0.0
            safe = jnp.where(pore, c[h], 1.0)
            both = 1.0 / (d * safe)
            g = RELAX * c[h] * (both * safe)
            G[X, h] = g * c[h]
            S[X, h] = g * strided(rn, X - 1, h)
            if own:
                rc = jnp.where(pore, both * d, 0.0)
                RC[X, h] = rc
                W[X, h] = (1.0 / RELAX) * d * rc
                zacc[lax.div(X - XO, 8), h] += edge(c[h]) * c[h][4]

    def sweep(src, X):
        u, near = around(src, X)
        return [0.2 * u[h] + (S[X, h] + G[X, h] * near[h]) for h in range(2)]

    def first(X):
        for h, v in enumerate(sweep(S, X)):
            UA[X, h] = v

    def second(X):
        for h, v in enumerate(sweep(UA, X)):
            UB[X, h] = jnp.where(inside, v, 0.0)

    def resid(X):
        u, near = around(UB, X)
        slab = lax.div(X - XO, 8)
        for h in range(2):
            racc[slab, h] += W[X, h] * (S[X, h] - RELAX * u[h] + G[X, h] * near[h])
            tacc[slab, h] += edge(cs[X, h]) * u[h][4]

    def run(fn, lo, hi, step=8):
        whole = (hi - lo) // step

        def body(i, _):
            for j in range(step):
                fn(lo + XO + i * step + j)
            return 0

        if whole:
            lax.fori_loop(0, whole, body, 0)
        for x in range(lo + whole * step, hi):
            fn(x + XO)

    own_setup = functools.partial(setup, own=True)
    for n in range(NCH):
        for cp in ymsg[n]:
            cp.wait()
        unpack(n)
        run(own_setup, max(CH * n - 1, 1), CH * n + CH - 1, CH)
    run(first, 2, 22, 7)
    run(second, 3, 21, 6)
    run(resid, 4, 20, 8)

    for cp in xmsg + cmsg:
        cp.wait()
    for X, side in ((0, left), (1, left), (2, left), (27, right), (28, right), (29, right)):
        for h in range(2):
            cs[X, h] = strided(cn, X, h) * side
    for n, (dr, db) in enumerate(CORNERS):
        side = (left if dr < 0 else right) * (below if db < 0 else above)
        for p in range(2):
            X = (1 + p) if dr < 0 else (27 + p)
            for h in range(2):
                for j in range(2):
                    v = crecv[n, (p * 2 + h) * 2 + j] * side
                    if db < 0:
                        cs[X, h, 2 + j, 0:1, :] = v
                    else:
                        cs[X, h, 5 + j, 7:8, :] = v
        X, y = (1 if dr < 0 else 26), (7 if db < 0 else 72)
        for h in range(2):
            rn[X, h, y : y + 1, :] = crecv[n, 8 + h]
    for x in (-2, -1, 0, 23, 24, 25):
        setup(x + XO, 0 <= x < XL)
    for x in (-1, 0, 1, 22, 23, 24):
        first(x + XO)
    for x in (0, 1, 2, 21, 22, 23):
        second(x + XO)
    for x in (0, 1, 2, 3, 20, 21, 22, 23):
        resid(x + XO)

    parts = [halves(lambda h, s=s: y_total(racc[s, h])) for s in range(3)]
    parts += [halves(lambda h, s=s: tacc[s, h]) for s in range(3)]
    parts += [halves(lambda h: y_total(cs[2, h] * UB[3, h])), halves(lambda h: y_total(cs[27, h] * UB[26, h]))]
    parts += [halves(lambda h, s=s: zacc[s, h]) for s in range(3)]
    parts += [faces(2), faces(26)]
    tot = dot(jnp.concatenate(parts, axis=0), pz[...])
    tot = [tot[8 * i : 8 * i + 8] for i in range(13)]
    group = lax.div(iota(1), 32)
    ends = [tot[6], zero8, tot[7]]
    for s in range(3):
        RM[7 + s, 1] = jnp.where(
            group == 0, tot[s], jnp.where(group == 1, tot[3 + s], jnp.where(group == 2, ends[s], 0.0))
        )
    rmsg = [
        remote(RM.at[7:10, 1], RM.at[7 - 3 * dr : 10 - 3 * dr, 1 - db], (dr, db)) for dr, db in NEAR
    ]
    for dr, db in FAR:
        s, t = (9, 0) if dr > 0 else (7, 16)
        rmsg.append(remote(RM.at[s, 1], RM.at[t, 1 - db], (dr, db)))

    cxs = [tot[11], EC[6], EC[7], tot[12]]
    for s in range(3):
        face = tot[8 + s]
        cx, cx2, cy, cz = cxs[s], cxs[s + 1], EC[3 + s] + jnp.where(sub == 0, face, 0.0), EC[8 + s]
        cy2 = jnp.where(sub == 7, face, pltpu.roll(cy, 7, 0))
        diag = MASS * (EC[s] + 1.0) + cx + cx2 + cy + cy2 + cz + pltpu.roll(cz, 127, 1)
        CM[6 + s, 1] = jnp.where(
            group == 0, RELAX / diag, jnp.where(group == 1, cx, jnp.where(group == 2, cy, cz))
        )
    kmsg = [
        remote(CM.at[6:9, 1], CM.at[6 - 3 * dr : 9 - 3 * dr, 1 - db], (dr, db)) for dr, db in NEAR
    ]

    def upack(x, _):
        for h in range(2):
            for j in range(3):
                usend[0, (x * 2 + h) * 3 + j] = UB[x + XO, h, 4 + j, 0:1, :]
                usend[1, (x * 2 + h) * 3 + j] = UB[x + XO, h, 2 + j, 7:8, :]
        return 0

    lax.fori_loop(0, XL, upack, 0)
    for n, (dr, db) in enumerate(CORNERS):
        for p in range(2):
            X = XO + (p if dr < 0 else XL - 2 + p)
            for h in range(2):
                for j in range(2):
                    at = (p * 2 + h) * 2 + j
                    vsend[n, at] = UB[X, h, 4 + j, 0:1, :] if db < 0 else UB[X, h, 3 + j, 7:8, :]
    uymsg = [remote(usend.at[0], urecv.at[1], (0, -1)), remote(usend.at[1], urecv.at[0], (0, 1))]
    uxmsg = [remote(UB.at[3:6], xhalo.at[1], (-1, 0)), remote(UB.at[24:27], xhalo.at[0], (1, 0))]
    ucmsg = [remote(vsend.at[n], vrecv.at[3 - n], off) for n, off in enumerate(CORNERS)]

    def turned(v, groups):
        return pltpu.roll(v, groups % 4 * 32, v.ndim - 1) if groups % 4 else v

    def gather(msgs, g):
        out = jnp.where(group == 2, turned(msgs[2], 2 - g), 0.0)
        out = jnp.where(group == 1, turned(msgs[1], 1 - g), out)
        return jnp.where(group == 0, turned(msgs[0], -g), out)

    def down_y(v):
        t = pltpu.roll(v, 1, v.ndim - 2)
        return jnp.where(sub == 0, turned(t, 1), t)

    def up_y(v):
        t = pltpu.roll(v, 7, v.ndim - 2)
        return jnp.where(sub == 7, turned(t, -1), t)

    for cp in kmsg:
        cp.wait()

    msgs = [CM[:, i] for i in range(3)]
    q = gather(msgs, 0)
    cx = gather(msgs, 1)
    cy = gather(msgs, 2)
    cz = gather(msgs, 3)
    CO[:, 0] = q
    CO[:, 1] = q * cx
    CO[0:14, 2] = q[0:14] * cx[1:15]
    CO[:, 3] = q * cy
    CO[:, 4] = q * up_y(cy)
    CO[:, 5] = q * cz
    CO[:, 6] = q * jnp.where(group < 3, pltpu.roll(cz, 127, 2), 0.0)

    for cp in uymsg + uxmsg + ucmsg:
        cp.wait()

    def uunpack(x, _):
        for h in range(2):
            for j in range(3):
                UB[x + XO, h, 1 + j, 0:1, :] = urecv[0, (x * 2 + h) * 3 + j] * below
                UB[x + XO, h, 5 + j, 7:8, :] = urecv[1, (x * 2 + h) * 3 + j] * above
        return 0

    lax.fori_loop(0, XL, uunpack, 0)
    for X, n, i, side in (
        (0, 0, 0, left), (1, 0, 1, left), (2, 0, 2, left),
        (27, 1, 0, right), (28, 1, 1, right), (29, 1, 2, right),
    ):
        for h in range(2):
            UB[X, h] = xhalo[n, i, h] * side
    for n, (dr, db) in enumerate(CORNERS):
        side = (left if dr < 0 else right) * (below if db < 0 else above)
        for p in range(2):
            X = (1 + p) if dr < 0 else (27 + p)
            for h in range(2):
                for j in range(2):
                    v = vrecv[n, (p * 2 + h) * 2 + j] * side
                    if db < 0:
                        UB[X, h, 2 + j, 0:1, :] = v
                    else:
                        UB[X, h, 5 + j, 7:8, :] = v

    for cp in rmsg:
        cp.wait()

    msgs = [RM[:, i] for i in range(3)]
    res = gather([m[1:16] for m in msgs], 0)
    face = gather([m[1:16] for m in msgs], 1)
    res = res + jnp.where(sub == 0, down_y(face), jnp.where(sub == 7, up_y(face), 0.0))
    face = gather(msgs, 2)
    start = []
    for s in range(15):
        v = res[s]
        if s % 3 == 0:
            v = v + face[s]
        if s % 3 == 2:
            v = v + face[s + 2]
        v = CO[s, 0] * v
        RO[s] = v
        start.append(v)
    e = dict(enumerate(start))
    for it in range(1, 6):
        new = {}
        for s in range(it, 15 - it):
            v = e[s]
            off = CO[s, 1] * e[s - 1] + CO[s, 2] * e[s + 1]
            off = off + CO[s, 3] * down_y(v) + CO[s, 4] * up_y(v)
            off = off + CO[s, 5] * pltpu.roll(v, 1, 1) + CO[s, 6] * pltpu.roll(v, 127, 1)
            new[s] = 0.2 * v + (RO[s] + off)
        e = new
    parts = []
    for s in range(5, 10):
        parts += [e[s], down_y(e[s]), up_y(e[s])]
    wide = dot(jnp.concatenate(parts, axis=0), px[...])

    for s in range(5):
        for h in range(2):
            mid, dn, up = (wide[24 * s + 8 * i : 24 * s + 8 * i + 8, 128 * h : 128 * h + 128] for i in range(3))
            lay = []
            for i in range(YV):
                v = mid
                if i < 4:
                    v = jnp.where(sub < 4 - i, dn, v)
                elif i > 4:
                    v = jnp.where(sub >= 12 - i, up, v)
                lay.append(v)
            lay = jnp.stack(lay, axis=0)
            lo, hi = ((0, 3), (3, 11), (11, 19), (19, 27), (27, 30))[s]

            def add(X, _, lay=lay, h=h):
                UA[X, h] = UB[X, h] + cs[X, h] * lay
                return 0

            lax.fori_loop(lo, hi, add, 0)

    def third(X):
        for h, v in enumerate(sweep(UA, X)):
            UB[X, h] = v

    def fourth(X):
        for h, v in enumerate(sweep(UB, X)):
            UA[X, h] = v

    def fifth(X):
        for h, v in enumerate(sweep(UA, X)):
            v = v * RC[X, h]
            for i in range(YV):
                on[X - XO, h, pl.ds(4 + i, 8, stride=9), :] = v[i]

    run(third, -2, 26, 7)
    run(fourth, -1, 25, 13)
    outs = []
    for n in range(4):
        run(fifth, 6 * n, 6 * n + 6, 6)
        for h in range(2):
            cp = pltpu.make_async_copy(
                on.at[6 * n : 6 * n + 6, h, 8:72, :],
                out_ref.at[6 * n : 6 * n + 6, :, pl.ds(128 * h, 128)],
                out_sem.at[2 * n + h],
            )
            cp.start()
            outs.append(cp)
    for cp in outs:
        cp.wait()


def vmem(*shape):
    return pltpu.VMEM(shape, F32)


def shards(right_side, knudsen, solid):
    n_msg = 2 * NCH + 8 + 20 + 14 + 8
    scratch = [
        vmem(XL, 64, 256), pltpu.VMEM((XL, 64, 256), jnp.int32), vmem(30, 2, 80, 128), vmem(28, 2, 80, 128),
    ]
    scratch += [vmem(30, 2, YV, 8, 128) for _ in range(7)]
    scratch += [vmem(XL, 2, 80, 128)]
    scratch += [vmem(2, NCH, CH * 10, 1, 128), vmem(2, NCH, CH * 10, 1, 128), vmem(4, 10, 1, 128), vmem(4, 10, 1, 128)]
    scratch += [vmem(2, 144, 1, 128), vmem(2, 144, 1, 128), vmem(4, 8, 1, 128), vmem(4, 8, 1, 128)]
    scratch += [vmem(2, 3, 2, YV, 8, 128)]
    scratch += [
        vmem(3, 2, YV, 8, 128), vmem(3, 2, 8, 128), vmem(3, 2, YV, 8, 128), vmem(3, 2, YV, 8, 128),
        vmem(3, 2, YV, 8, 128), vmem(3, 2, 8, 128),
    ]
    scratch += [vmem(15, 3, 8, 128), vmem(17, 3, 8, 128), vmem(15, 7, 8, 128), vmem(15, 8, 128)]
    scratch += [vmem(256, 128), vmem(128, 256), vmem(256, 128), vmem(XL, 64, 256), vmem(11, 8, 128)]
    scratch += [
        pltpu.SemaphoreType.DMA((3 * NCH,)), pltpu.SemaphoreType.DMA((8,)),
        pltpu.SemaphoreType.DMA((n_msg,)), pltpu.SemaphoreType.DMA((n_msg,)),
    ]
    return pl.pallas_call(
        kernel,
        name="vcycle",
        out_shape=pltpu.VMEM(right_side.shape, F32),
        in_specs=[pl.BlockSpec(memory_space=pltpu.HBM)] * 3,
        out_specs=pl.BlockSpec(memory_space=pltpu.VMEM),
        scratch_shapes=scratch,
        compiler_params=pltpu.CompilerParams(
            collective_id=0, has_side_effects=True, vmem_limit_bytes=58 * 2**20
        ),
    )(knudsen, solid, right_side)


def solution(mesh):
    placed = P("region", "block", None)
    return jax.shard_map(shards, mesh=mesh, in_specs=(placed,) * 3, out_specs=placed, check_vma=False)
```

```python
import functools

import jax
import jax.numpy as jnp
from jax import lax
from jax.experimental import pallas as pl
from jax.experimental.pallas import tpu as pltpu
from jax.sharding import PartitionSpec as P

MESH = pl.DeviceIdType.MESH
F32 = jnp.float32
NREG, NBLK = 32, 8
XL = 24
YV = 9
XO = 3
NCH, CH = 4, 6
CROWS = CH * 6
MASS = 0.05
RELAX = 0.8

NEAR = [(dr, db) for dr in (-2, -1, 0, 1, 2) for db in (-1, 0, 1) if (dr, db) != (0, 0)]
FAR = [(dr, db) for dr in (-3, 3) for db in (-1, 0, 1)]
CORNERS = [(dr, db) for dr in (-1, 1) for db in (-1, 1)]


def iota(axis, shape=(8, 128)):
    return lax.broadcasted_iota(jnp.int32, shape, axis)


def z_sides(a, b):
    lane = iota(2, (1, 8, 128))
    first, last = lane == 0, lane == 127
    ra, rb = pltpu.roll(a, 1, 2), pltpu.roll(b, 1, 2)
    la, lb = pltpu.roll(a, 127, 2), pltpu.roll(b, 127, 2)
    low = (jnp.where(first, 0.0, ra), jnp.where(first, ra, rb))
    high = (jnp.where(last, lb, la), jnp.where(last, 0.0, lb))
    return low, high


def y_sides(a):
    down = jnp.concatenate([pltpu.roll(a[YV - 1 :], 1, 1), a[: YV - 1]], axis=0)
    up = jnp.concatenate([a[1:], pltpu.roll(a[:1], 7, 1)], axis=0)
    return down, up


def around(ref, X):
    a, b = ref[X, 0], ref[X, 1]
    low, high = z_sides(a, b)
    out = []
    for h, v in ((0, a), (1, b)):
        down, up = y_sides(v)
        out.append((low[h] + high[h]) + (down + up) + (ref[X - 1, h] + ref[X + 1, h]))
    return (a, b), out


def y_total(v):
    sub = iota(0)
    same, less, more = None, None, None
    for i in range(YV):
        lo, hi = 4 - i, 12 - i
        s = v[i]
        if i < 4:
            t = jnp.where((sub < lo) & (sub > 0), s, 0.0)
            less = t if less is None else less + t
            s = jnp.where(sub >= lo, s, 0.0)
        elif i > 4:
            t = jnp.where((sub >= hi) & (sub < 7), s, 0.0)
            more = t if more is None else more + t
            s = jnp.where(sub < hi, s, 0.0)
        same = s if same is None else same + s
    return same + pltpu.roll(less, 7, 0) + pltpu.roll(more, 1, 0)


def dot(a, b):
    return jnp.dot(a, b, precision=lax.Precision.HIGHEST, preferred_element_type=F32)


def kernel(
    k_ref, solid_ref, rs_ref, out_ref,
    kn, sn, cn, rn, cs, S, G, W, RC, UA, UB, on,
    ysend, yrecv, csend, crecv, usend, urecv, vsend, vrecv, xhalo,
    racc, tacc, cnt, czacc, cyacc, zacc, CM, RM, CO, RO, pz, px, po,
    rsn, EC, wide, LAY, UC, load_sem, out_sem, ss, rr,
):
    r = lax.axis_index("region")
    b = lax.axis_index("block")

    def dev(dr, db):
        return (lax.rem(r + (dr + NREG), NREG), lax.rem(b + (db + NBLK), NBLK))

    bar = pltpu.get_barrier_semaphore()
    for off in NEAR + FAR:
        pl.semaphore_signal(bar, inc=1, device_id=dev(*off), device_id_type=MESH)

    loads = []
    for n in range(NCH):
        part = pl.ds(n * CH, CH)
        for i, (src, dst) in enumerate(((k_ref, kn), (solid_ref, sn), (rs_ref, rsn))):
            cp = pltpu.make_async_copy(src.at[part], dst.at[part], load_sem.at[3 * n + i])
            cp.start()
            loads.append(cp)

    row, col = iota(0, (256, 128)), iota(1, (256, 128))
    cell = lax.rem(col, 32)
    pz[...] = jnp.where(lax.div(row, 8) == cell, 1.0, 0.0)
    po[...] = jnp.where(row == 8 * cell, 1.0, 0.0)
    row, col = iota(0, (128, 256)), iota(1, (128, 256))
    px[...] = jnp.where(row - 32 == lax.div(col, 8), 1.0, 0.0)
    zero8 = jnp.zeros((8, 128), F32)
    zeros9 = jnp.zeros((YV, 8, 128), F32)

    def clear(x, _):
        for h in range(2):
            cn[x, h, 0:8, :] = zero8
            cn[x, h, 72:80, :] = zero8
            rn[jnp.minimum(x, XL + 3), h, 0:8, :] = zero8
            rn[jnp.minimum(x, XL + 3), h, 72:80, :] = zero8
        return 0

    lax.fori_loop(0, XL + 2 * XO, clear, 0)
    for h in range(2):
        UB[XO - 1, h] = zeros9
        UB[XO + XL, h] = zeros9
        for s in range(3):
            for ref in (racc, cnt, czacc, cyacc):
                ref[s, h] = zeros9
            for ref in (tacc, zacc):
                ref[s, h] = zero8

    count = [0]

    def remote(src, dst, off):
        n = count[0]
        count[0] += 1
        cp = pltpu.make_async_remote_copy(
            src_ref=src, dst_ref=dst, send_sem=ss.at[n], recv_sem=rr.at[n],
            device_id=dev(*off), device_id_type=MESH,
        )
        cp.start()
        return cp

    ymsg = []
    for n in range(NCH):
        for cp in loads[3 * n : 3 * n + 3]:
            cp.wait()

        def root(i, _, n=n):
            x = n * CH + i
            for h in range(2):
                half = slice(128 * h, 128 * h + 128)
                k = kn[x, :, half]
                cn[x + XO, h, 8:72, :] = jnp.where(sn[x, :, half] == 0, k * lax.rsqrt(k), 0.0)
                rn[x + 2, h, 8:72, :] = rsn[x, :, half]
                for side in range(2):
                    for j in range(3):
                        y = j if side == 0 else 61 + j
                        ysend[side, n, (i * 2 + h) * 3 + j] = cn[x + XO, h, 8 + y : 9 + y, :]
                    for j in range(2):
                        y = j if side == 0 else 62 + j
                        ysend[side, n, CROWS + (i * 2 + h) * 2 + j] = rn[x + 2, h, 8 + y : 9 + y, :]
            return 0

        lax.fori_loop(0, CH, root, 0, unroll=2)
        if n == 0:
            pl.semaphore_wait(bar, len(NEAR) + len(FAR))
        ymsg.append([
            remote(ysend.at[0, n], yrecv.at[1, n], (0, -1)), remote(ysend.at[1, n], yrecv.at[0, n], (0, 1))
        ])

    for n, (dr, db) in enumerate(CORNERS):
        for p in range(2):
            x = p if dr < 0 else XL - 2 + p
            for h in range(2):
                for j in range(2):
                    y = j if db < 0 else 62 + j
                    csend[n, (p * 2 + h) * 2 + j] = cn[x + XO, h, 8 + y : 9 + y, :]
        x, y = 0 if dr < 0 else XL - 1, 0 if db < 0 else 63
        for h in range(2):
            csend[n, 8 + h] = rn[x + 2, h, 8 + y : 9 + y, :]
    xmsg = [
        remote(cn.at[3:6, :, 8:72, :], cn.at[27:30, :, 8:72, :], (-1, 0)),
        remote(cn.at[24:27, :, 8:72, :], cn.at[0:3, :, 8:72, :], (1, 0)),
        remote(rn.at[2:4, :, 8:72, :], rn.at[26:28, :, 8:72, :], (-1, 0)),
        remote(rn.at[24:26, :, 8:72, :], rn.at[0:2, :, 8:72, :], (1, 0)),
    ]
    cmsg = [remote(csend.at[n], crecv.at[3 - n], off) for n, off in enumerate(CORNERS)]

    def strided(ref, X, h):
        return jnp.stack([ref[X, h, pl.ds(4 + i, 8, stride=9), :] for i in range(YV)], axis=0)

    def deal(x, _):
        X = x + XO
        c = [strided(cn, X, h) for h in range(2)]
        low, _high = z_sides(*c)
        slab = lax.div(x, 8)
        for h in range(2):
            cs[X, h] = c[h]
            cnt[slab, h] += jnp.where(c[h] > 0.0, 1.0, 0.0)
            czacc[slab, h] += c[h] * low[h]
            cyacc[slab, h] += c[h] * y_sides(c[h])[0]
        return 0

    lax.fori_loop(0, XL, deal, 0, unroll=4)

    vec, subs = iota(0, (YV, 8, 128)), iota(1, (YV, 8, 128))
    place = subs * YV + vec
    inside = (place >= 4) & (place < 68)
    turn = lax.rem(vec + subs, 8) == 4

    def halves(fn):
        return jnp.concatenate([fn(0), fn(1)], axis=1)

    def faces(X):
        return halves(lambda h: y_total(cs[X, h] * cs[X + 1, h]))

    def early_sums():
        parts = [halves(lambda h, s=s: y_total(cnt[s, h])) for s in range(3)]
        parts += [halves(lambda h, s=s: y_total(jnp.where(turn, cyacc[s, h], 0.0))) for s in range(3)]
        parts += [faces(10), faces(18)]
        early = dot(jnp.concatenate(parts, axis=0), pz[...])
        for i in range(8):
            EC[i] = early[8 * i : 8 * i + 8]
        early = dot(jnp.concatenate([halves(lambda h, s=s: y_total(czacc[s, h])) for s in range(3)], axis=0), po[...])
        for i in range(3):
            EC[8 + i] = early[8 * i : 8 * i + 8]

    early_sums()

    below = jnp.where(b > 0, 1.0, 0.0).astype(F32)
    above = jnp.where(b < NBLK - 1, 1.0, 0.0).astype(F32)
    left = jnp.where(r > 0, 1.0, 0.0).astype(F32)
    right = jnp.where(r < NREG - 1, 1.0, 0.0).astype(F32)

    sub = iota(0)

    def edge(v):
        return jnp.where(sub == 0, v[3], jnp.where(sub == 7, v[5], 0.0))

    def unpack(n):
        def body(i, _):
            x = n * CH + i
            for h in range(2):
                at = (i * 2 + h) * 3
                for j in range(3):
                    cs[x + XO, h, 1 + j, 0:1, :] = yrecv[0, n, at + j] * below
                    cs[x + XO, h, 5 + j, 7:8, :] = yrecv[1, n, at + j] * above
                at = CROWS + (i * 2 + h) * 2
                for j in range(2):
                    rn[x + 2, h, 6 + j : 7 + j, :] = yrecv[0, n, at + j]
                    rn[x + 2, h, 72 + j : 73 + j, :] = yrecv[1, n, at + j]
                zacc[lax.div(x, 8), h] += edge(cs[x + XO, h]) * cs[x + XO, h, 4]
            return 0

        lax.fori_loop(0, CH, body, 0, unroll=2)

    def setup(X, own):
        c, near = around(cs, X)
        for h in range(2):
            d = MASS + c[h] * near[h]
            pore = c[h] > 0.0
            safe = jnp.where(pore, c[h], 1.0)
            both = 1.0 / (d * safe)
            g = RELAX * c[h] * (both * safe)
            G[X, h] = g * c[h]
            S[X, h] = g * strided(rn, X - 1, h)
            if own:
                rc = jnp.where(pore, both * d, 0.0)
                RC[X, h] = rc
                W[X, h] = (1.0 / RELAX) * d * rc

    def sweep(src, X):
        u, near = around(src, X)
        return [0.2 * u[h] + (S[X, h] + G[X, h] * near[h]) for h in range(2)]

    def first(X):
        for h, v in enumerate(sweep(S, X)):
            UA[X, h] = v

    def second(X):
        for h, v in enumerate(sweep(UA, X)):
            UB[X, h] = jnp.where(inside, v, 0.0)

    def resid(X):
        u, near = around(UB, X)
        slab = lax.div(X - XO, 8)
        for h in range(2):
            racc[slab, h] += W[X, h] * (S[X, h] - RELAX * u[h] + G[X, h] * near[h])
            tacc[slab, h] += edge(cs[X, h]) * u[h][4]

    def run(fn, lo, hi, step=8):
        whole = (hi - lo) // step

        def body(i, _):
            for j in range(step):
                fn(lo + XO + i * step + j)
            return 0

        if whole:
            lax.fori_loop(0, whole, body, 0)
        for x in range(lo + whole * step, hi):
            fn(x + XO)

    own_setup = functools.partial(setup, own=True)
    for n in range(NCH):
        for cp in ymsg[n]:
            cp.wait()
        unpack(n)
        run(own_setup, max(CH * n - 1, 1), CH * n + CH - 1, CH)
    run(first, 2, 22, 7)
    run(second, 3, 21, 6)
    run(resid, 4, 20, 8)

    for cp in xmsg + cmsg:
        cp.wait()
    def x_halo():
        for X, side in ((0, left), (1, left), (2, left), (27, right), (28, right), (29, right)):
            for h in range(2):
                cs[X, h] = strided(cn, X, h) * side
        for n, (dr, db) in enumerate(CORNERS):
            side = (left if dr < 0 else right) * (below if db < 0 else above)
            for p in range(2):
                X = (1 + p) if dr < 0 else (27 + p)
                for h in range(2):
                    for j in range(2):
                        v = crecv[n, (p * 2 + h) * 2 + j] * side
                        if db < 0:
                            cs[X, h, 2 + j, 0:1, :] = v
                        else:
                            cs[X, h, 5 + j, 7:8, :] = v
            X, y = (1 if dr < 0 else 26), (7 if db < 0 else 72)
            for h in range(2):
                rn[X, h, y : y + 1, :] = crecv[n, 8 + h]

    x_halo()
    group = lax.div(iota(1), 32)

    def conductances():
        parts = [halves(lambda h, s=s: zacc[s, h]) for s in range(3)] + [faces(2), faces(26)]
        tot = dot(jnp.concatenate(parts, axis=0), pz[...])
        tot = [tot[8 * i : 8 * i + 8] for i in range(5)]
        cxs = [tot[3], EC[6], EC[7], tot[4]]
        for s in range(3):
            face = tot[s]
            cx, cx2, cy, cz = cxs[s], cxs[s + 1], EC[3 + s] + jnp.where(sub == 0, face, 0.0), EC[8 + s]
            cy2 = jnp.where(sub == 7, face, pltpu.roll(cy, 7, 0))
            diag = MASS * (EC[s] + 1.0) + cx + cx2 + cy + cy2 + cz + pltpu.roll(cz, 127, 1)
            CM[6 + s, 1] = jnp.where(
                group == 0, RELAX / diag, jnp.where(group == 1, cx, jnp.where(group == 2, cy, cz))
            )

    conductances()
    kmsg = [
        remote(CM.at[6:9, 1], CM.at[6 - 3 * dr : 9 - 3 * dr, 1 - db], (dr, db)) for dr, db in NEAR
    ]

    def ends():
        for x in (-2, -1, 0, 23, 24, 25):
            setup(x + XO, 0 <= x < XL)
        for x in (-1, 0, 1, 22, 23, 24):
            first(x + XO)
        for x in (0, 1, 2, 21, 22, 23):
            second(x + XO)
        for x in (0, 1, 2, 3, 20, 21, 22, 23):
            resid(x + XO)

    ends()

    def residual_sums():
        parts = [halves(lambda h, s=s: y_total(racc[s, h])) for s in range(3)]
        parts += [halves(lambda h, s=s: tacc[s, h]) for s in range(3)]
        parts += [halves(lambda h: y_total(cs[2, h] * UB[3, h])), halves(lambda h: y_total(cs[27, h] * UB[26, h]))]
        tot = dot(jnp.concatenate(parts, axis=0), pz[...])
        tot = [tot[8 * i : 8 * i + 8] for i in range(8)]
        end = [tot[6], zero8, tot[7]]
        for s in range(3):
            RM[7 + s, 1] = jnp.where(
                group == 0, tot[s], jnp.where(group == 1, tot[3 + s], jnp.where(group == 2, end[s], 0.0))
            )

    residual_sums()
    rmsg = [
        remote(RM.at[7:10, 1], RM.at[7 - 3 * dr : 10 - 3 * dr, 1 - db], (dr, db)) for dr, db in NEAR
    ]
    for dr, db in FAR:
        s, t = (9, 0) if dr > 0 else (7, 16)
        rmsg.append(remote(RM.at[s, 1], RM.at[t, 1 - db], (dr, db)))

    def upack(x, _):
        for h in range(2):
            for j in range(3):
                usend[0, (x * 2 + h) * 3 + j] = UB[x + XO, h, 4 + j, 0:1, :]
                usend[1, (x * 2 + h) * 3 + j] = UB[x + XO, h, 2 + j, 7:8, :]
        return 0

    lax.fori_loop(0, XL, upack, 0)
    for n, (dr, db) in enumerate(CORNERS):
        for p in range(2):
            X = XO + (p if dr < 0 else XL - 2 + p)
            for h in range(2):
                for j in range(2):
                    at = (p * 2 + h) * 2 + j
                    vsend[n, at] = UB[X, h, 4 + j, 0:1, :] if db < 0 else UB[X, h, 3 + j, 7:8, :]
    uymsg = [remote(usend.at[0], urecv.at[1], (0, -1)), remote(usend.at[1], urecv.at[0], (0, 1))]
    uxmsg = [remote(UB.at[3:6], xhalo.at[1], (-1, 0)), remote(UB.at[24:27], xhalo.at[0], (1, 0))]
    ucmsg = [remote(vsend.at[n], vrecv.at[3 - n], off) for n, off in enumerate(CORNERS)]

    def turned(v, groups):
        return pltpu.roll(v, groups % 4 * 32, v.ndim - 1) if groups % 4 else v

    def gather(msgs, g):
        out = jnp.where(group == 2, turned(msgs[2], 2 - g), 0.0)
        out = jnp.where(group == 1, turned(msgs[1], 1 - g), out)
        return jnp.where(group == 0, turned(msgs[0], -g), out)

    def down_y(v):
        t = pltpu.roll(v, 1, v.ndim - 2)
        return jnp.where(sub == 0, turned(t, 1), t)

    def up_y(v):
        t = pltpu.roll(v, 7, v.ndim - 2)
        return jnp.where(sub == 7, turned(t, -1), t)

    for cp in kmsg:
        cp.wait()

    def coefficients():
        msgs = [CM[:, i] for i in range(3)]
        q = gather(msgs, 0)
        cx = gather(msgs, 1)
        cy = gather(msgs, 2)
        cz = gather(msgs, 3)
        CO[:, 0] = q
        CO[:, 1] = q * cx
        CO[0:14, 2] = q[0:14] * cx[1:15]
        CO[:, 3] = q * cy
        CO[:, 4] = q * up_y(cy)
        CO[:, 5] = q * cz
        CO[:, 6] = q * jnp.where(group < 3, pltpu.roll(cz, 127, 2), 0.0)

    coefficients()

    for cp in uymsg + uxmsg + ucmsg:
        cp.wait()

    def uunpack(x, _):
        for h in range(2):
            for j in range(3):
                UB[x + XO, h, 1 + j, 0:1, :] = urecv[0, (x * 2 + h) * 3 + j] * below
                UB[x + XO, h, 5 + j, 7:8, :] = urecv[1, (x * 2 + h) * 3 + j] * above
        return 0

    lax.fori_loop(0, XL, uunpack, 0)
    def u_halo():
        for X, n, i, side in (
            (0, 0, 0, left), (1, 0, 1, left), (2, 0, 2, left),
            (27, 1, 0, right), (28, 1, 1, right), (29, 1, 2, right),
        ):
            for h in range(2):
                UB[X, h] = xhalo[n, i, h] * side
        for n, (dr, db) in enumerate(CORNERS):
            side = (left if dr < 0 else right) * (below if db < 0 else above)
            for p in range(2):
                X = (1 + p) if dr < 0 else (27 + p)
                for h in range(2):
                    for j in range(2):
                        v = vrecv[n, (p * 2 + h) * 2 + j] * side
                        if db < 0:
                            UB[X, h, 2 + j, 0:1, :] = v
                        else:
                            UB[X, h, 5 + j, 7:8, :] = v

    u_halo()

    for cp in rmsg:
        cp.wait()

    def solve():
        msgs = [RM[:, i] for i in range(3)]
        res = gather([m[1:16] for m in msgs], 0)
        face = gather([m[1:16] for m in msgs], 1)
        res = res + jnp.where(sub == 0, down_y(face), jnp.where(sub == 7, up_y(face), 0.0))
        face = gather(msgs, 2)
        start = []
        for s in range(15):
            v = res[s]
            if s % 3 == 0:
                v = v + face[s]
            if s % 3 == 2:
                v = v + face[s + 2]
            v = CO[s, 0] * v
            RO[s] = v
            start.append(v)
        e = dict(enumerate(start))
        for it in range(1, 6):
            new = {}
            for s in range(it, 15 - it):
                v = e[s]
                off = CO[s, 1] * e[s - 1] + CO[s, 2] * e[s + 1]
                off = off + CO[s, 3] * down_y(v) + CO[s, 4] * up_y(v)
                off = off + CO[s, 5] * pltpu.roll(v, 1, 1) + CO[s, 6] * pltpu.roll(v, 127, 1)
                new[s] = 0.2 * v + (RO[s] + off)
            e = new
        parts = []
        for s in range(5, 10):
            parts += [e[s], down_y(e[s]), up_y(e[s])]
        wide[...] = dot(jnp.concatenate(parts, axis=0), px[...])

    solve()

    for s in range(5):
        for h in range(2):
            mid, dn, up = (wide[24 * s + 8 * i : 24 * s + 8 * i + 8, 128 * h : 128 * h + 128] for i in range(3))
            lay = []
            for i in range(YV):
                v = mid
                if i < 4:
                    v = jnp.where(sub < 4 - i, dn, v)
                elif i > 4:
                    v = jnp.where(sub >= 12 - i, up, v)
                lay.append(v)
            lay = jnp.stack(lay, axis=0)
            LAY[s, h] = lay

    def add(X):
        for h in range(2):
            UA[X, h] = UB[X, h] + cs[X, h] * LAY[lax.div(X + 5, 8), h]

    def third(X):
        add(X + 1)
        for h, v in enumerate(sweep(UA, X)):
            UC[X, h] = v

    def fourth(X):
        for h, v in enumerate(sweep(UC, X)):
            UA[X, h] = v

    def fifth(X):
        for h, v in enumerate(sweep(UA, X)):
            v = v * RC[X, h]
            for i in range(YV):
                on[X - XO, h, pl.ds(4 + i, 8, stride=9), :] = v[i]

    add(0)
    add(1)
    run(third, -2, 26, 7)
    run(fourth, -1, 25, 13)
    outs = []
    for n in range(4):
        run(fifth, 6 * n, 6 * n + 6, 6)
        for h in range(2):
            cp = pltpu.make_async_copy(
                on.at[6 * n : 6 * n + 6, h, 8:72, :],
                out_ref.at[6 * n : 6 * n + 6, :, pl.ds(128 * h, 128)],
                out_sem.at[2 * n + h],
            )
            cp.start()
            outs.append(cp)
    for cp in outs:
        cp.wait()


def vmem(*shape):
    return pltpu.VMEM(shape, F32)


def shards(right_side, knudsen, solid):
    n_msg = 2 * NCH + 8 + 20 + 14 + 8
    scratch = [
        vmem(XL, 64, 256), pltpu.VMEM((XL, 64, 256), jnp.int32), vmem(30, 2, 80, 128), vmem(28, 2, 80, 128),
    ]
    scratch += [vmem(30, 2, YV, 8, 128) for _ in range(7)]
    scratch += [vmem(XL, 2, 80, 128)]
    scratch += [vmem(2, NCH, CH * 10, 1, 128), vmem(2, NCH, CH * 10, 1, 128), vmem(4, 10, 1, 128), vmem(4, 10, 1, 128)]
    scratch += [vmem(2, 144, 1, 128), vmem(2, 144, 1, 128), vmem(4, 8, 1, 128), vmem(4, 8, 1, 128)]
    scratch += [vmem(2, 3, 2, YV, 8, 128)]
    scratch += [
        vmem(3, 2, YV, 8, 128), vmem(3, 2, 8, 128), vmem(3, 2, YV, 8, 128), vmem(3, 2, YV, 8, 128),
        vmem(3, 2, YV, 8, 128), vmem(3, 2, 8, 128),
    ]
    scratch += [vmem(15, 3, 8, 128), vmem(17, 3, 8, 128), vmem(15, 7, 8, 128), vmem(15, 8, 128)]
    scratch += [vmem(256, 128), vmem(128, 256), vmem(256, 128), vmem(XL, 64, 256), vmem(11, 8, 128), vmem(120, 256), vmem(5, 2, YV, 8, 128), vmem(30, 2, YV, 8, 128)]
    scratch += [
        pltpu.SemaphoreType.DMA((3 * NCH,)), pltpu.SemaphoreType.DMA((8,)),
        pltpu.SemaphoreType.DMA((n_msg,)), pltpu.SemaphoreType.DMA((n_msg,)),
    ]
    return pl.pallas_call(
        kernel,
        name="vcycle",
        out_shape=pltpu.VMEM(right_side.shape, F32),
        in_specs=[pl.BlockSpec(memory_space=pltpu.HBM)] * 3,
        out_specs=pl.BlockSpec(memory_space=pltpu.VMEM),
        scratch_shapes=scratch,
        compiler_params=pltpu.CompilerParams(
            collective_id=0, has_side_effects=True, vmem_limit_bytes=58 * 2**20
        ),
    )(knudsen, solid, right_side)


def solution(mesh):
    placed = P("region", "block", None)
    return jax.shard_map(shards, mesh=mesh, in_specs=(placed,) * 3, out_specs=placed, check_vma=False)
```

```python
import functools

import jax
import jax.numpy as jnp
from jax import lax
from jax.experimental import pallas as pl
from jax.experimental.pallas import tpu as pltpu
from jax.sharding import PartitionSpec as P

MESH = pl.DeviceIdType.MESH
F32 = jnp.float32
NREG, NBLK = 32, 8
XL = 24
YV = 9
XO = 3
NCH, CH = 4, 6
CROWS = CH * 6
MASS = 0.05
RELAX = 0.8

NEAR = [(dr, db) for dr in (-2, -1, 0, 1, 2) for db in (-1, 0, 1) if (dr, db) != (0, 0)]
FAR = [(dr, db) for dr in (-3, 3) for db in (-1, 0, 1)]
CORNERS = [(dr, db) for dr in (-1, 1) for db in (-1, 1)]


def iota(axis, shape=(8, 128)):
    return lax.broadcasted_iota(jnp.int32, shape, axis)


def z_sides(a, b):
    lane = iota(2, (1, 8, 128))
    first, last = lane == 0, lane == 127
    ra, rb = pltpu.roll(a, 1, 2), pltpu.roll(b, 1, 2)
    la, lb = pltpu.roll(a, 127, 2), pltpu.roll(b, 127, 2)
    low = (jnp.where(first, 0.0, ra), jnp.where(first, ra, rb))
    high = (jnp.where(last, lb, la), jnp.where(last, 0.0, lb))
    return low, high


def y_sides(a):
    down = jnp.concatenate([pltpu.roll(a[YV - 1 :], 1, 1), a[: YV - 1]], axis=0)
    up = jnp.concatenate([a[1:], pltpu.roll(a[:1], 7, 1)], axis=0)
    return down, up


def around(ref, X):
    a, b = ref[X, 0], ref[X, 1]
    low, high = z_sides(a, b)
    out = []
    for h, v in ((0, a), (1, b)):
        down, up = y_sides(v)
        out.append((low[h] + high[h]) + (down + up) + (ref[X - 1, h] + ref[X + 1, h]))
    return (a, b), out


def y_total(v):
    sub = iota(0)
    same, less, more = None, None, None
    for i in range(YV):
        lo, hi = 4 - i, 12 - i
        s = v[i]
        if i < 4:
            t = jnp.where((sub < lo) & (sub > 0), s, 0.0)
            less = t if less is None else less + t
            s = jnp.where(sub >= lo, s, 0.0)
        elif i > 4:
            t = jnp.where((sub >= hi) & (sub < 7), s, 0.0)
            more = t if more is None else more + t
            s = jnp.where(sub < hi, s, 0.0)
        same = s if same is None else same + s
    return same + pltpu.roll(less, 7, 0) + pltpu.roll(more, 1, 0)


def dot(a, b):
    return jnp.dot(a, b, precision=lax.Precision.HIGHEST, preferred_element_type=F32)


def kernel(
    k_ref, solid_ref, rs_ref, out_ref,
    kn, sn, cn, rn, cs, S, G, W, RC, UA, UB, on,
    ysend, yrecv, csend, crecv, usend, urecv, vsend, vrecv, xhalo,
    racc, tacc, cnt, czacc, cyacc, zacc, CM, RM, CO, RO, pz, px, po,
    rsn, EC, wide, LAY, UC, load_sem, ss, rr,
):
    r = lax.axis_index("region")
    b = lax.axis_index("block")

    def dev(dr, db):
        return (lax.rem(r + (dr + NREG), NREG), lax.rem(b + (db + NBLK), NBLK))

    bar = pltpu.get_barrier_semaphore()
    for off in NEAR + FAR:
        pl.semaphore_signal(bar, inc=1, device_id=dev(*off), device_id_type=MESH)

    loads = []
    for n in range(NCH):
        part = pl.ds(n * CH, CH)
        for i, (src, dst) in enumerate(((k_ref, kn), (solid_ref, sn), (rs_ref, rsn))):
            cp = pltpu.make_async_copy(src.at[part], dst.at[part], load_sem.at[3 * n + i])
            cp.start()
            loads.append(cp)

    row, col = iota(0, (256, 128)), iota(1, (256, 128))
    cell = lax.rem(col, 32)
    pz[...] = jnp.where(lax.div(row, 8) == cell, 1.0, 0.0)
    po[...] = jnp.where(row == 8 * cell, 1.0, 0.0)
    row, col = iota(0, (128, 256)), iota(1, (128, 256))
    px[...] = jnp.where(row - 32 == lax.div(col, 8), 1.0, 0.0)
    zero8 = jnp.zeros((8, 128), F32)
    zeros9 = jnp.zeros((YV, 8, 128), F32)

    def clear(x, _):
        for h in range(2):
            cn[x, h, 0:8, :] = zero8
            cn[x, h, 72:80, :] = zero8
            rn[jnp.minimum(x, XL + 3), h, 0:8, :] = zero8
            rn[jnp.minimum(x, XL + 3), h, 72:80, :] = zero8
        return 0

    lax.fori_loop(0, XL + 2 * XO, clear, 0)
    for h in range(2):
        UB[XO - 1, h] = zeros9
        UB[XO + XL, h] = zeros9
        for s in range(3):
            for ref in (racc, cnt, czacc, cyacc):
                ref[s, h] = zeros9
            for ref in (tacc, zacc):
                ref[s, h] = zero8

    count = [0]

    def remote(src, dst, off):
        n = count[0]
        count[0] += 1
        cp = pltpu.make_async_remote_copy(
            src_ref=src, dst_ref=dst, send_sem=ss.at[n], recv_sem=rr.at[n],
            device_id=dev(*off), device_id_type=MESH,
        )
        cp.start()
        return cp

    ymsg = []
    for n in range(NCH):
        for cp in loads[3 * n : 3 * n + 3]:
            cp.wait()

        def root(i, _, n=n):
            x = n * CH + i
            for h in range(2):
                half = slice(128 * h, 128 * h + 128)
                k = kn[x, :, half]
                cn[x + XO, h, 8:72, :] = jnp.where(sn[x, :, half] == 0, k * lax.rsqrt(k), 0.0)
                rn[x + 2, h, 8:72, :] = rsn[x, :, half]
                for side in range(2):
                    for j in range(3):
                        y = j if side == 0 else 61 + j
                        ysend[side, n, (i * 2 + h) * 3 + j] = cn[x + XO, h, 8 + y : 9 + y, :]
                    for j in range(2):
                        y = j if side == 0 else 62 + j
                        ysend[side, n, CROWS + (i * 2 + h) * 2 + j] = rn[x + 2, h, 8 + y : 9 + y, :]
            return 0

        lax.fori_loop(0, CH, root, 0, unroll=2)
        if n == 0:
            pl.semaphore_wait(bar, len(NEAR) + len(FAR))
        ymsg.append([
            remote(ysend.at[0, n], yrecv.at[1, n], (0, -1)), remote(ysend.at[1, n], yrecv.at[0, n], (0, 1))
        ])

    for n, (dr, db) in enumerate(CORNERS):
        for p in range(2):
            x = p if dr < 0 else XL - 2 + p
            for h in range(2):
                for j in range(2):
                    y = j if db < 0 else 62 + j
                    csend[n, (p * 2 + h) * 2 + j] = cn[x + XO, h, 8 + y : 9 + y, :]
        x, y = 0 if dr < 0 else XL - 1, 0 if db < 0 else 63
        for h in range(2):
            csend[n, 8 + h] = rn[x + 2, h, 8 + y : 9 + y, :]
    xmsg = [
        remote(cn.at[3:6, :, 8:72, :], cn.at[27:30, :, 8:72, :], (-1, 0)),
        remote(cn.at[24:27, :, 8:72, :], cn.at[0:3, :, 8:72, :], (1, 0)),
        remote(rn.at[2:4, :, 8:72, :], rn.at[26:28, :, 8:72, :], (-1, 0)),
        remote(rn.at[24:26, :, 8:72, :], rn.at[0:2, :, 8:72, :], (1, 0)),
    ]
    cmsg = [remote(csend.at[n], crecv.at[3 - n], off) for n, off in enumerate(CORNERS)]

    def strided(ref, X, h):
        return jnp.stack([ref[X, h, pl.ds(4 + i, 8, stride=9), :] for i in range(YV)], axis=0)

    def deal(x, _):
        X = x + XO
        c = [strided(cn, X, h) for h in range(2)]
        low, _high = z_sides(*c)
        slab = lax.div(x, 8)
        for h in range(2):
            cs[X, h] = c[h]
            cnt[slab, h] += jnp.where(c[h] > 0.0, 1.0, 0.0)
            czacc[slab, h] += c[h] * low[h]
            cyacc[slab, h] += c[h] * y_sides(c[h])[0]
        return 0

    lax.fori_loop(0, XL, deal, 0, unroll=4)

    vec, subs = iota(0, (YV, 8, 128)), iota(1, (YV, 8, 128))
    place = subs * YV + vec
    inside = (place >= 4) & (place < 68)
    turn = lax.rem(vec + subs, 8) == 4

    def halves(fn):
        return jnp.concatenate([fn(0), fn(1)], axis=1)

    def faces(X):
        return halves(lambda h: y_total(cs[X, h] * cs[X + 1, h]))

    def early_sums():
        parts = [halves(lambda h, s=s: y_total(cnt[s, h])) for s in range(3)]
        parts += [halves(lambda h, s=s: y_total(jnp.where(turn, cyacc[s, h], 0.0))) for s in range(3)]
        parts += [faces(10), faces(18)]
        early = dot(jnp.concatenate(parts, axis=0), pz[...])
        for i in range(8):
            EC[i] = early[8 * i : 8 * i + 8]
        early = dot(jnp.concatenate([halves(lambda h, s=s: y_total(czacc[s, h])) for s in range(3)], axis=0), po[...])
        for i in range(3):
            EC[8 + i] = early[8 * i : 8 * i + 8]

    early_sums()

    below = jnp.where(b > 0, 1.0, 0.0).astype(F32)
    above = jnp.where(b < NBLK - 1, 1.0, 0.0).astype(F32)
    left = jnp.where(r > 0, 1.0, 0.0).astype(F32)
    right = jnp.where(r < NREG - 1, 1.0, 0.0).astype(F32)

    sub = iota(0)

    def edge(v):
        return jnp.where(sub == 0, v[3], jnp.where(sub == 7, v[5], 0.0))

    def unpack(n):
        def body(i, _):
            x = n * CH + i
            for h in range(2):
                at = (i * 2 + h) * 3
                for j in range(3):
                    cs[x + XO, h, 1 + j, 0:1, :] = yrecv[0, n, at + j] * below
                    cs[x + XO, h, 5 + j, 7:8, :] = yrecv[1, n, at + j] * above
                at = CROWS + (i * 2 + h) * 2
                for j in range(2):
                    rn[x + 2, h, 6 + j : 7 + j, :] = yrecv[0, n, at + j]
                    rn[x + 2, h, 72 + j : 73 + j, :] = yrecv[1, n, at + j]
                zacc[lax.div(x, 8), h] += edge(cs[x + XO, h]) * cs[x + XO, h, 4]
            return 0

        lax.fori_loop(0, CH, body, 0, unroll=2)

    def setup(X, own):
        c, near = around(cs, X)
        for h in range(2):
            d = MASS + c[h] * near[h]
            pore = c[h] > 0.0
            safe = jnp.where(pore, c[h], 1.0)
            both = 1.0 / (d * safe)
            g = RELAX * c[h] * (both * safe)
            G[X, h] = g * c[h]
            S[X, h] = g * strided(rn, X - 1, h)
            if own:
                rc = jnp.where(pore, both * d, 0.0)
                RC[X, h] = rc
                W[X, h] = (1.0 / RELAX) * d * rc

    def sweep(src, X):
        u, near = around(src, X)
        return [0.2 * u[h] + (S[X, h] + G[X, h] * near[h]) for h in range(2)]

    def first(X):
        for h, v in enumerate(sweep(S, X)):
            UA[X, h] = v

    def second(X):
        for h, v in enumerate(sweep(UA, X)):
            UB[X, h] = jnp.where(inside, v, 0.0)

    def resid(X):
        u, near = around(UB, X)
        slab = lax.div(X - XO, 8)
        for h in range(2):
            racc[slab, h] += W[X, h] * (S[X, h] - RELAX * u[h] + G[X, h] * near[h])
            tacc[slab, h] += edge(cs[X, h]) * u[h][4]

    def run(fn, lo, hi, step=8):
        whole = (hi - lo) // step

        def body(i, _):
            for j in range(step):
                fn(lo + XO + i * step + j)
            return 0

        if whole:
            lax.fori_loop(0, whole, body, 0)
        for x in range(lo + whole * step, hi):
            fn(x + XO)

    own_setup = functools.partial(setup, own=True)
    for n in range(NCH):
        for cp in ymsg[n]:
            cp.wait()
        unpack(n)
        run(own_setup, max(CH * n - 1, 1), CH * n + CH - 1, CH)
    run(first, 2, 22, 7)
    run(second, 3, 21, 6)
    run(resid, 4, 20, 8)

    for cp in xmsg + cmsg:
        cp.wait()
    def x_halo():
        for X, side in ((0, left), (1, left), (2, left), (27, right), (28, right), (29, right)):
            for h in range(2):
                cs[X, h] = strided(cn, X, h) * side
        for n, (dr, db) in enumerate(CORNERS):
            side = (left if dr < 0 else right) * (below if db < 0 else above)
            for p in range(2):
                X = (1 + p) if dr < 0 else (27 + p)
                for h in range(2):
                    for j in range(2):
                        v = crecv[n, (p * 2 + h) * 2 + j] * side
                        if db < 0:
                            cs[X, h, 2 + j, 0:1, :] = v
                        else:
                            cs[X, h, 5 + j, 7:8, :] = v
            X, y = (1 if dr < 0 else 26), (7 if db < 0 else 72)
            for h in range(2):
                rn[X, h, y : y + 1, :] = crecv[n, 8 + h]

    x_halo()
    group = lax.div(iota(1), 32)

    def conductances():
        parts = [halves(lambda h, s=s: zacc[s, h]) for s in range(3)] + [faces(2), faces(26)]
        tot = dot(jnp.concatenate(parts, axis=0), pz[...])
        tot = [tot[8 * i : 8 * i + 8] for i in range(5)]
        cxs = [tot[3], EC[6], EC[7], tot[4]]
        for s in range(3):
            face = tot[s]
            cx, cx2, cy, cz = cxs[s], cxs[s + 1], EC[3 + s] + jnp.where(sub == 0, face, 0.0), EC[8 + s]
            cy2 = jnp.where(sub == 7, face, pltpu.roll(cy, 7, 0))
            diag = MASS * (EC[s] + 1.0) + cx + cx2 + cy + cy2 + cz + pltpu.roll(cz, 127, 1)
            CM[6 + s, 1] = jnp.where(
                group == 0, RELAX / diag, jnp.where(group == 1, cx, jnp.where(group == 2, cy, cz))
            )

    conductances()
    kmsg = [
        remote(CM.at[6:9, 1], CM.at[6 - 3 * dr : 9 - 3 * dr, 1 - db], (dr, db)) for dr, db in NEAR
    ]

    def ends():
        for x in (-2, -1, 0, 23, 24, 25):
            setup(x + XO, 0 <= x < XL)
        for x in (-1, 0, 1, 22, 23, 24):
            first(x + XO)
        for x in (0, 1, 2, 21, 22, 23):
            second(x + XO)
        for x in (0, 1, 2, 3, 20, 21, 22, 23):
            resid(x + XO)

    ends()

    def residual_sums():
        parts = [halves(lambda h, s=s: y_total(racc[s, h])) for s in range(3)]
        parts += [halves(lambda h, s=s: tacc[s, h]) for s in range(3)]
        parts += [halves(lambda h: y_total(cs[2, h] * UB[3, h])), halves(lambda h: y_total(cs[27, h] * UB[26, h]))]
        tot = dot(jnp.concatenate(parts, axis=0), pz[...])
        tot = [tot[8 * i : 8 * i + 8] for i in range(8)]
        end = [tot[6], zero8, tot[7]]
        for s in range(3):
            RM[7 + s, 1] = jnp.where(
                group == 0, tot[s], jnp.where(group == 1, tot[3 + s], jnp.where(group == 2, end[s], 0.0))
            )

    residual_sums()
    rmsg = [
        remote(RM.at[7:10, 1], RM.at[7 - 3 * dr : 10 - 3 * dr, 1 - db], (dr, db)) for dr, db in NEAR
    ]
    for dr, db in FAR:
        s, t = (9, 0) if dr > 0 else (7, 16)
        rmsg.append(remote(RM.at[s, 1], RM.at[t, 1 - db], (dr, db)))

    def upack(x, _):
        for h in range(2):
            for j in range(3):
                usend[0, (x * 2 + h) * 3 + j] = UB[x + XO, h, 4 + j, 0:1, :]
                usend[1, (x * 2 + h) * 3 + j] = UB[x + XO, h, 2 + j, 7:8, :]
        return 0

    lax.fori_loop(0, XL, upack, 0)
    for n, (dr, db) in enumerate(CORNERS):
        for p in range(2):
            X = XO + (p if dr < 0 else XL - 2 + p)
            for h in range(2):
                for j in range(2):
                    at = (p * 2 + h) * 2 + j
                    vsend[n, at] = UB[X, h, 4 + j, 0:1, :] if db < 0 else UB[X, h, 3 + j, 7:8, :]
    uymsg = [remote(usend.at[0], urecv.at[1], (0, -1)), remote(usend.at[1], urecv.at[0], (0, 1))]
    uxmsg = [remote(UB.at[3:6], xhalo.at[1], (-1, 0)), remote(UB.at[24:27], xhalo.at[0], (1, 0))]
    ucmsg = [remote(vsend.at[n], vrecv.at[3 - n], off) for n, off in enumerate(CORNERS)]

    def turned(v, groups):
        return pltpu.roll(v, groups % 4 * 32, v.ndim - 1) if groups % 4 else v

    def gather(msgs, g):
        out = jnp.where(group == 2, turned(msgs[2], 2 - g), 0.0)
        out = jnp.where(group == 1, turned(msgs[1], 1 - g), out)
        return jnp.where(group == 0, turned(msgs[0], -g), out)

    def down_y(v):
        t = pltpu.roll(v, 1, v.ndim - 2)
        return jnp.where(sub == 0, turned(t, 1), t)

    def up_y(v):
        t = pltpu.roll(v, 7, v.ndim - 2)
        return jnp.where(sub == 7, turned(t, -1), t)

    for cp in kmsg:
        cp.wait()

    def coefficients():
        msgs = [CM[:, i] for i in range(3)]
        q = gather(msgs, 0)
        cx = gather(msgs, 1)
        cy = gather(msgs, 2)
        cz = gather(msgs, 3)
        CO[:, 0] = q
        CO[:, 1] = q * cx
        CO[0:14, 2] = q[0:14] * cx[1:15]
        CO[:, 3] = q * cy
        CO[:, 4] = q * up_y(cy)
        CO[:, 5] = q * cz
        CO[:, 6] = q * jnp.where(group < 3, pltpu.roll(cz, 127, 2), 0.0)

    coefficients()

    for cp in uxmsg:
        cp.wait_send()
    for cp in uymsg:
        cp.wait()

    def uunpack(x, _):
        for h in range(2):
            for j in range(3):
                UB[x + XO, h, 1 + j, 0:1, :] = urecv[0, (x * 2 + h) * 3 + j] * below
                UB[x + XO, h, 5 + j, 7:8, :] = urecv[1, (x * 2 + h) * 3 + j] * above
        return 0

    lax.fori_loop(0, XL, uunpack, 0)
    def u_halo():
        for X, n, i, side in (
            (0, 0, 0, left), (1, 0, 1, left), (2, 0, 2, left),
            (27, 1, 0, right), (28, 1, 1, right), (29, 1, 2, right),
        ):
            for h in range(2):
                UB[X, h] = xhalo[n, i, h] * side
        for n, (dr, db) in enumerate(CORNERS):
            side = (left if dr < 0 else right) * (below if db < 0 else above)
            for p in range(2):
                X = (1 + p) if dr < 0 else (27 + p)
                for h in range(2):
                    for j in range(2):
                        v = vrecv[n, (p * 2 + h) * 2 + j] * side
                        if db < 0:
                            UB[X, h, 2 + j, 0:1, :] = v
                        else:
                            UB[X, h, 5 + j, 7:8, :] = v

    for cp in rmsg:
        cp.wait()

    def solve():
        msgs = [RM[:, i] for i in range(3)]
        res = gather([m[1:16] for m in msgs], 0)
        face = gather([m[1:16] for m in msgs], 1)
        res = res + jnp.where(sub == 0, down_y(face), jnp.where(sub == 7, up_y(face), 0.0))
        face = gather(msgs, 2)
        start = []
        for s in range(15):
            v = res[s]
            if s % 3 == 0:
                v = v + face[s]
            if s % 3 == 2:
                v = v + face[s + 2]
            v = CO[s, 0] * v
            RO[s] = v
            start.append(v)
        e = dict(enumerate(start))
        for it in range(1, 6):
            new = {}
            for s in range(it, 15 - it):
                v = e[s]
                off = CO[s, 1] * e[s - 1] + CO[s, 2] * e[s + 1]
                off = off + CO[s, 3] * down_y(v) + CO[s, 4] * up_y(v)
                off = off + CO[s, 5] * pltpu.roll(v, 1, 1) + CO[s, 6] * pltpu.roll(v, 127, 1)
                new[s] = 0.2 * v + (RO[s] + off)
            e = new
        parts = []
        for s in range(5, 10):
            parts += [e[s], down_y(e[s]), up_y(e[s])]
        wide[...] = dot(jnp.concatenate(parts, axis=0), px[...])

    solve()

    for cp in uxmsg:
        cp.wait_recv()
    for cp in ucmsg:
        cp.wait()
    u_halo()

    for s in range(5):
        for h in range(2):
            mid, dn, up = (wide[24 * s + 8 * i : 24 * s + 8 * i + 8, 128 * h : 128 * h + 128] for i in range(3))
            lay = []
            for i in range(YV):
                v = mid
                if i < 4:
                    v = jnp.where(sub < 4 - i, dn, v)
                elif i > 4:
                    v = jnp.where(sub >= 12 - i, up, v)
                lay.append(v)
            lay = jnp.stack(lay, axis=0)
            LAY[s, h] = lay

    def add(X):
        for h in range(2):
            UA[X, h] = UB[X, h] + cs[X, h] * LAY[lax.div(X + 5, 8), h]

    def third(X):
        add(X + 1)
        for h, v in enumerate(sweep(UA, X)):
            UC[X, h] = v

    def fourth(X):
        for h, v in enumerate(sweep(UC, X)):
            UA[X, h] = v

    def fifth(X):
        for h, v in enumerate(sweep(UA, X)):
            v = v * RC[X, h]
            for i in range(YV):
                on[X - XO, h, pl.ds(4 + i, 8, stride=9), :] = v[i]
            out_ref[X - XO, :, 128 * h : 128 * h + 128] = on[X - XO, h, 8:72, :]

    add(0)
    add(1)
    run(third, -2, 26, 7)
    run(fourth, -1, 25, 13)
    run(fifth, 0, XL, 8)


def vmem(*shape):
    return pltpu.VMEM(shape, F32)


def shards(right_side, knudsen, solid):
    n_msg = 2 * NCH + 8 + 20 + 14 + 8
    scratch = [
        vmem(XL, 64, 256), pltpu.VMEM((XL, 64, 256), jnp.int32), vmem(30, 2, 80, 128), vmem(28, 2, 80, 128),
    ]
    scratch += [vmem(30, 2, YV, 8, 128) for _ in range(7)]
    scratch += [vmem(XL, 2, 80, 128)]
    scratch += [vmem(2, NCH, CH * 10, 1, 128), vmem(2, NCH, CH * 10, 1, 128), vmem(4, 10, 1, 128), vmem(4, 10, 1, 128)]
    scratch += [vmem(2, 144, 1, 128), vmem(2, 144, 1, 128), vmem(4, 8, 1, 128), vmem(4, 8, 1, 128)]
    scratch += [vmem(2, 3, 2, YV, 8, 128)]
    scratch += [
        vmem(3, 2, YV, 8, 128), vmem(3, 2, 8, 128), vmem(3, 2, YV, 8, 128), vmem(3, 2, YV, 8, 128),
        vmem(3, 2, YV, 8, 128), vmem(3, 2, 8, 128),
    ]
    scratch += [vmem(15, 3, 8, 128), vmem(17, 3, 8, 128), vmem(15, 7, 8, 128), vmem(15, 8, 128)]
    scratch += [vmem(256, 128), vmem(128, 256), vmem(256, 128), vmem(XL, 64, 256), vmem(11, 8, 128), vmem(120, 256), vmem(5, 2, YV, 8, 128), vmem(30, 2, YV, 8, 128)]
    scratch += [
        pltpu.SemaphoreType.DMA((3 * NCH,)),
        pltpu.SemaphoreType.DMA((n_msg,)), pltpu.SemaphoreType.DMA((n_msg,)),
    ]
    return pl.pallas_call(
        kernel,
        name="vcycle",
        out_shape=pltpu.VMEM(right_side.shape, F32),
        in_specs=[pl.BlockSpec(memory_space=pltpu.HBM)] * 3,
        out_specs=pl.BlockSpec(memory_space=pltpu.VMEM),
        scratch_shapes=scratch,
        compiler_params=pltpu.CompilerParams(
            collective_id=0, has_side_effects=True, vmem_limit_bytes=58 * 2**20
        ),
    )(knudsen, solid, right_side)


def solution(mesh):
    placed = P("region", "block", None)
    return jax.shard_map(shards, mesh=mesh, in_specs=(placed,) * 3, out_specs=placed, check_vma=False)
```

```python
import functools

import jax
import jax.numpy as jnp
from jax import lax
from jax.experimental import pallas as pl
from jax.experimental.pallas import tpu as pltpu
from jax.sharding import PartitionSpec as P

MESH = pl.DeviceIdType.MESH
F32 = jnp.float32
NREG, NBLK = 32, 8
XL = 24
YV = 9
XO = 3
NCH, CH = 4, 6
CROWS = CH * 6
MASS = 0.05
RELAX = 0.8

NEAR = [(dr, db) for dr in (-2, 2, -1, 1, 0) for db in (-1, 1, 0) if (dr, db) != (0, 0)]
FAR = [(dr, db) for dr in (-3, 3) for db in (-1, 0, 1)]
CORNERS = [(dr, db) for dr in (-1, 1) for db in (-1, 1)]


def iota(axis, shape=(8, 128)):
    return lax.broadcasted_iota(jnp.int32, shape, axis)


def z_sides(a, b):
    lane = iota(2, (1, 8, 128))
    first, last = lane == 0, lane == 127
    ra, rb = pltpu.roll(a, 1, 2), pltpu.roll(b, 1, 2)
    la, lb = pltpu.roll(a, 127, 2), pltpu.roll(b, 127, 2)
    low = (jnp.where(first, 0.0, ra), jnp.where(first, ra, rb))
    high = (jnp.where(last, lb, la), jnp.where(last, 0.0, lb))
    return low, high


def y_sides(a):
    down = jnp.concatenate([pltpu.roll(a[YV - 1 :], 1, 1), a[: YV - 1]], axis=0)
    up = jnp.concatenate([a[1:], pltpu.roll(a[:1], 7, 1)], axis=0)
    return down, up


def around(ref, X):
    a, b = ref[X, 0], ref[X, 1]
    low, high = z_sides(a, b)
    out = []
    for h, v in ((0, a), (1, b)):
        down, up = y_sides(v)
        out.append((low[h] + high[h]) + (down + up) + (ref[X - 1, h] + ref[X + 1, h]))
    return (a, b), out


def y_total(v):
    sub = iota(0)
    same, less, more = None, None, None
    for i in range(YV):
        lo, hi = 4 - i, 12 - i
        s = v[i]
        if i < 4:
            t = jnp.where((sub < lo) & (sub > 0), s, 0.0)
            less = t if less is None else less + t
            s = jnp.where(sub >= lo, s, 0.0)
        elif i > 4:
            t = jnp.where((sub >= hi) & (sub < 7), s, 0.0)
            more = t if more is None else more + t
            s = jnp.where(sub < hi, s, 0.0)
        same = s if same is None else same + s
    return same + pltpu.roll(less, 7, 0) + pltpu.roll(more, 1, 0)


def dot(a, b):
    return jnp.dot(a, b, precision=lax.Precision.HIGHEST, preferred_element_type=F32)


def kernel(
    k_ref, solid_ref, rs_ref, out_ref,
    kn, sn, cn, rn, cs, S, G, W, RC, UA, UB, on,
    ysend, yrecv, csend, crecv, usend, urecv, vsend, vrecv, xhalo,
    racc, tacc, cnt, czacc, cyacc, zacc, CM, RM, CO, RO, pz, px, po,
    rsn, EC, wide, LAY, UC, load_sem, ss, rr,
):
    r = lax.axis_index("region")
    b = lax.axis_index("block")

    def dev(dr, db):
        return (lax.rem(r + (dr + NREG), NREG), lax.rem(b + (db + NBLK), NBLK))

    bar = pltpu.get_barrier_semaphore()
    for off in FAR + NEAR:
        pl.semaphore_signal(bar, inc=1, device_id=dev(*off), device_id_type=MESH)

    loads = []
    for n in range(NCH):
        part = pl.ds(n * CH, CH)
        for i, (src, dst) in enumerate(((k_ref, kn), (solid_ref, sn), (rs_ref, rsn))):
            cp = pltpu.make_async_copy(src.at[part], dst.at[part], load_sem.at[3 * n + i])
            cp.start()
            loads.append(cp)

    row, col = iota(0, (256, 128)), iota(1, (256, 128))
    cell = lax.rem(col, 32)
    pz[...] = jnp.where(lax.div(row, 8) == cell, 1.0, 0.0)
    po[...] = jnp.where(row == 8 * cell, 1.0, 0.0)
    row, col = iota(0, (128, 256)), iota(1, (128, 256))
    px[...] = jnp.where(row - 32 == lax.div(col, 8), 1.0, 0.0)
    zero8 = jnp.zeros((8, 128), F32)
    zeros9 = jnp.zeros((YV, 8, 128), F32)

    def clear(x, _):
        for h in range(2):
            cn[x, h, 0:8, :] = zero8
            cn[x, h, 72:80, :] = zero8
            rn[jnp.minimum(x, XL + 3), h, 0:8, :] = zero8
            rn[jnp.minimum(x, XL + 3), h, 72:80, :] = zero8
        return 0

    lax.fori_loop(0, XL + 2 * XO, clear, 0)
    for h in range(2):
        UB[XO - 1, h] = zeros9
        UB[XO + XL, h] = zeros9
        for s in range(3):
            for ref in (racc, cnt, czacc, cyacc):
                ref[s, h] = zeros9
            for ref in (tacc, zacc):
                ref[s, h] = zero8

    count = [0]

    def remote(src, dst, off):
        n = count[0]
        count[0] += 1
        cp = pltpu.make_async_remote_copy(
            src_ref=src, dst_ref=dst, send_sem=ss.at[n], recv_sem=rr.at[n],
            device_id=dev(*off), device_id_type=MESH,
        )
        cp.start()
        return cp

    ymsg = []
    for n in range(NCH):
        for cp in loads[3 * n : 3 * n + 3]:
            cp.wait()

        def root(i, _, n=n):
            x = n * CH + i
            for h in range(2):
                half = slice(128 * h, 128 * h + 128)
                k = kn[x, :, half]
                cn[x + XO, h, 8:72, :] = jnp.where(sn[x, :, half] == 0, k * lax.rsqrt(k), 0.0)
                rn[x + 2, h, 8:72, :] = rsn[x, :, half]
                for side in range(2):
                    for j in range(3):
                        y = j if side == 0 else 61 + j
                        ysend[side, n, (i * 2 + h) * 3 + j] = cn[x + XO, h, 8 + y : 9 + y, :]
                    for j in range(2):
                        y = j if side == 0 else 62 + j
                        ysend[side, n, CROWS + (i * 2 + h) * 2 + j] = rn[x + 2, h, 8 + y : 9 + y, :]
            return 0

        lax.fori_loop(0, CH, root, 0, unroll=3)
        if n == 0:
            pl.semaphore_wait(bar, len(NEAR) + len(FAR))
        ymsg.append([
            remote(ysend.at[0, n], yrecv.at[1, n], (0, -1)), remote(ysend.at[1, n], yrecv.at[0, n], (0, 1))
        ])

    for n, (dr, db) in enumerate(CORNERS):
        for p in range(2):
            x = p if dr < 0 else XL - 2 + p
            for h in range(2):
                for j in range(2):
                    y = j if db < 0 else 62 + j
                    csend[n, (p * 2 + h) * 2 + j] = cn[x + XO, h, 8 + y : 9 + y, :]
        x, y = 0 if dr < 0 else XL - 1, 0 if db < 0 else 63
        for h in range(2):
            csend[n, 8 + h] = rn[x + 2, h, 8 + y : 9 + y, :]
    xmsg = [
        remote(cn.at[3:6, :, 8:72, :], cn.at[27:30, :, 8:72, :], (-1, 0)),
        remote(cn.at[24:27, :, 8:72, :], cn.at[0:3, :, 8:72, :], (1, 0)),
        remote(rn.at[2:4, :, 8:72, :], rn.at[26:28, :, 8:72, :], (-1, 0)),
        remote(rn.at[24:26, :, 8:72, :], rn.at[0:2, :, 8:72, :], (1, 0)),
    ]
    cmsg = [remote(csend.at[n], crecv.at[3 - n], off) for n, off in enumerate(CORNERS)]

    def strided(ref, X, h):
        return jnp.stack([ref[X, h, pl.ds(4 + i, 8, stride=9), :] for i in range(YV)], axis=0)

    def deal(x, _):
        X = x + XO
        c = [strided(cn, X, h) for h in range(2)]
        low, _high = z_sides(*c)
        slab = lax.div(x, 8)
        for h in range(2):
            cs[X, h] = c[h]
            cnt[slab, h] += jnp.where(c[h] > 0.0, 1.0, 0.0)
            czacc[slab, h] += c[h] * low[h]
            cyacc[slab, h] += c[h] * y_sides(c[h])[0]
        return 0

    lax.fori_loop(0, XL, deal, 0, unroll=4)

    vec, subs = iota(0, (YV, 8, 128)), iota(1, (YV, 8, 128))
    place = subs * YV + vec
    inside = (place >= 4) & (place < 68)
    turn = lax.rem(vec + subs, 8) == 4

    def halves(fn):
        return jnp.concatenate([fn(0), fn(1)], axis=1)

    def faces(X):
        return halves(lambda h: y_total(cs[X, h] * cs[X + 1, h]))

    def early_sums():
        parts = [halves(lambda h, s=s: y_total(cnt[s, h])) for s in range(3)]
        parts += [halves(lambda h, s=s: y_total(jnp.where(turn, cyacc[s, h], 0.0))) for s in range(3)]
        parts += [faces(10), faces(18)]
        early = dot(jnp.concatenate(parts, axis=0), pz[...])
        for i in range(8):
            EC[i] = early[8 * i : 8 * i + 8]
        early = dot(jnp.concatenate([halves(lambda h, s=s: y_total(czacc[s, h])) for s in range(3)], axis=0), po[...])
        for i in range(3):
            EC[8 + i] = early[8 * i : 8 * i + 8]

    early_sums()

    below = jnp.where(b > 0, 1.0, 0.0).astype(F32)
    above = jnp.where(b < NBLK - 1, 1.0, 0.0).astype(F32)
    left = jnp.where(r > 0, 1.0, 0.0).astype(F32)
    right = jnp.where(r < NREG - 1, 1.0, 0.0).astype(F32)

    sub = iota(0)

    def edge(v):
        return jnp.where(sub == 0, v[3], jnp.where(sub == 7, v[5], 0.0))

    def unpack(n):
        def body(i, _):
            x = n * CH + i
            for h in range(2):
                at = (i * 2 + h) * 3
                for j in range(3):
                    cs[x + XO, h, 1 + j, 0:1, :] = yrecv[0, n, at + j] * below
                    cs[x + XO, h, 5 + j, 7:8, :] = yrecv[1, n, at + j] * above
                at = CROWS + (i * 2 + h) * 2
                for j in range(2):
                    rn[x + 2, h, 6 + j : 7 + j, :] = yrecv[0, n, at + j]
                    rn[x + 2, h, 72 + j : 73 + j, :] = yrecv[1, n, at + j]
                zacc[lax.div(x, 8), h] += edge(cs[x + XO, h]) * cs[x + XO, h, 4]
            return 0

        lax.fori_loop(0, CH, body, 0, unroll=2)

    def setup(X, own):
        c, near = around(cs, X)
        for h in range(2):
            d = MASS + c[h] * near[h]
            pore = c[h] > 0.0
            safe = jnp.where(pore, c[h], 1.0)
            both = 1.0 / (d * safe)
            g = RELAX * c[h] * (both * safe)
            G[X, h] = g * c[h]
            S[X, h] = g * strided(rn, X - 1, h)
            if own:
                rc = jnp.where(pore, both * d, 0.0)
                RC[X, h] = rc
                W[X, h] = (1.0 / RELAX) * d * rc

    def sweep(src, X):
        u, near = around(src, X)
        return [0.2 * u[h] + (S[X, h] + G[X, h] * near[h]) for h in range(2)]

    def first(X):
        for h, v in enumerate(sweep(S, X)):
            UA[X, h] = v

    def second(X):
        for h, v in enumerate(sweep(UA, X)):
            UB[X, h] = jnp.where(inside, v, 0.0)

    def resid(X):
        u, near = around(UB, X)
        slab = lax.div(X - XO, 8)
        for h in range(2):
            racc[slab, h] += W[X, h] * (S[X, h] - RELAX * u[h] + G[X, h] * near[h])
            tacc[slab, h] += edge(cs[X, h]) * u[h][4]

    def run(fn, lo, hi, step=8):
        whole = (hi - lo) // step

        def body(i, _):
            for j in range(step):
                fn(lo + XO + i * step + j)
            return 0

        if whole:
            lax.fori_loop(0, whole, body, 0)
        for x in range(lo + whole * step, hi):
            fn(x + XO)

    own_setup = functools.partial(setup, own=True)
    for n in range(NCH):
        for cp in ymsg[n]:
            cp.wait()
        unpack(n)
        run(own_setup, max(CH * n - 1, 1), CH * n + CH - 1, CH)
    run(first, 2, 22, 10)
    run(second, 3, 21, 9)
    run(resid, 4, 20, 8)

    for cp in xmsg + cmsg:
        cp.wait()
    def x_halo():
        for X, side in ((0, left), (1, left), (2, left), (27, right), (28, right), (29, right)):
            for h in range(2):
                cs[X, h] = strided(cn, X, h) * side
        for n, (dr, db) in enumerate(CORNERS):
            side = (left if dr < 0 else right) * (below if db < 0 else above)
            for p in range(2):
                X = (1 + p) if dr < 0 else (27 + p)
                for h in range(2):
                    for j in range(2):
                        v = crecv[n, (p * 2 + h) * 2 + j] * side
                        if db < 0:
                            cs[X, h, 2 + j, 0:1, :] = v
                        else:
                            cs[X, h, 5 + j, 7:8, :] = v
            X, y = (1 if dr < 0 else 26), (7 if db < 0 else 72)
            for h in range(2):
                rn[X, h, y : y + 1, :] = crecv[n, 8 + h]

    x_halo()
    group = lax.div(iota(1), 32)

    def conductances():
        parts = [halves(lambda h, s=s: zacc[s, h]) for s in range(3)] + [faces(2), faces(26)]
        tot = dot(jnp.concatenate(parts, axis=0), pz[...])
        tot = [tot[8 * i : 8 * i + 8] for i in range(5)]
        cxs = [tot[3], EC[6], EC[7], tot[4]]
        for s in range(3):
            face = tot[s]
            cx, cx2, cy, cz = cxs[s], cxs[s + 1], EC[3 + s] + jnp.where(sub == 0, face, 0.0), EC[8 + s]
            cy2 = jnp.where(sub == 7, face, pltpu.roll(cy, 7, 0))
            diag = MASS * (EC[s] + 1.0) + cx + cx2 + cy + cy2 + cz + pltpu.roll(cz, 127, 1)
            CM[6 + s, 1] = jnp.where(
                group == 0, RELAX / diag, jnp.where(group == 1, cx, jnp.where(group == 2, cy, cz))
            )

    conductances()
    kmsg = [
        remote(CM.at[6:9, 1], CM.at[6 - 3 * dr : 9 - 3 * dr, 1 - db], (dr, db)) for dr, db in NEAR
    ]

    def ends():
        for x in (-2, -1, 0, 23, 24, 25):
            setup(x + XO, 0 <= x < XL)
        for x in (-1, 0, 1, 22, 23, 24):
            first(x + XO)
        for x in (0, 1, 2, 21, 22, 23):
            second(x + XO)
        for x in (0, 1, 2, 3, 20, 21, 22, 23):
            resid(x + XO)

    ends()

    def residual_sums():
        parts = [halves(lambda h, s=s: y_total(racc[s, h])) for s in range(3)]
        parts += [halves(lambda h, s=s: tacc[s, h]) for s in range(3)]
        parts += [halves(lambda h: y_total(cs[2, h] * UB[3, h])), halves(lambda h: y_total(cs[27, h] * UB[26, h]))]
        tot = dot(jnp.concatenate(parts, axis=0), pz[...])
        tot = [tot[8 * i : 8 * i + 8] for i in range(8)]
        end = [tot[6], zero8, tot[7]]
        for s in range(3):
            RM[7 + s, 1] = jnp.where(
                group == 0, tot[s], jnp.where(group == 1, tot[3 + s], jnp.where(group == 2, end[s], 0.0))
            )

    residual_sums()
    rmsg = []
    for dr, db in FAR:
        s, t = (9, 0) if dr > 0 else (7, 16)
        rmsg.append(remote(RM.at[s, 1], RM.at[t, 1 - db], (dr, db)))
    for dr, db in NEAR:
        rmsg.append(remote(RM.at[7:10, 1], RM.at[7 - 3 * dr : 10 - 3 * dr, 1 - db], (dr, db)))

    def upack(x, _):
        for h in range(2):
            for j in range(3):
                usend[0, (x * 2 + h) * 3 + j] = UB[x + XO, h, 4 + j, 0:1, :]
                usend[1, (x * 2 + h) * 3 + j] = UB[x + XO, h, 2 + j, 7:8, :]
        return 0

    lax.fori_loop(0, XL, upack, 0, unroll=4)
    for n, (dr, db) in enumerate(CORNERS):
        for p in range(2):
            X = XO + (p if dr < 0 else XL - 2 + p)
            for h in range(2):
                for j in range(2):
                    at = (p * 2 + h) * 2 + j
                    vsend[n, at] = UB[X, h, 4 + j, 0:1, :] if db < 0 else UB[X, h, 3 + j, 7:8, :]
    uymsg = [remote(usend.at[0], urecv.at[1], (0, -1)), remote(usend.at[1], urecv.at[0], (0, 1))]
    uxmsg = [remote(UB.at[3:6], xhalo.at[1], (-1, 0)), remote(UB.at[24:27], xhalo.at[0], (1, 0))]
    ucmsg = [remote(vsend.at[n], vrecv.at[3 - n], off) for n, off in enumerate(CORNERS)]

    def turned(v, groups):
        return pltpu.roll(v, groups % 4 * 32, v.ndim - 1) if groups % 4 else v

    def gather(msgs, g):
        out = jnp.where(group == 2, turned(msgs[2], 2 - g), 0.0)
        out = jnp.where(group == 1, turned(msgs[1], 1 - g), out)
        return jnp.where(group == 0, turned(msgs[0], -g), out)

    def down_y(v):
        t = pltpu.roll(v, 1, v.ndim - 2)
        return jnp.where(sub == 0, turned(t, 1), t)

    def up_y(v):
        t = pltpu.roll(v, 7, v.ndim - 2)
        return jnp.where(sub == 7, turned(t, -1), t)

    for cp in kmsg:
        cp.wait()

    def coefficients():
        msgs = [CM[:, i] for i in range(3)]
        q = gather(msgs, 0)
        cx = gather(msgs, 1)
        cy = gather(msgs, 2)
        cz = gather(msgs, 3)
        CO[:, 0] = q
        CO[:, 1] = q * cx
        CO[0:14, 2] = q[0:14] * cx[1:15]
        CO[:, 3] = q * cy
        CO[:, 4] = q * up_y(cy)
        CO[:, 5] = q * cz
        CO[:, 6] = q * jnp.where(group < 3, pltpu.roll(cz, 127, 2), 0.0)

    coefficients()

    for cp in uxmsg:
        cp.wait_send()
    for cp in uymsg:
        cp.wait()

    def uunpack(x, _):
        for h in range(2):
            for j in range(3):
                UB[x + XO, h, 1 + j, 0:1, :] = urecv[0, (x * 2 + h) * 3 + j] * below
                UB[x + XO, h, 5 + j, 7:8, :] = urecv[1, (x * 2 + h) * 3 + j] * above
        return 0

    lax.fori_loop(0, XL, uunpack, 0, unroll=4)
    def u_halo():
        for X, n, i, side in (
            (0, 0, 0, left), (1, 0, 1, left), (2, 0, 2, left),
            (27, 1, 0, right), (28, 1, 1, right), (29, 1, 2, right),
        ):
            for h in range(2):
                UB[X, h] = xhalo[n, i, h] * side
        for n, (dr, db) in enumerate(CORNERS):
            side = (left if dr < 0 else right) * (below if db < 0 else above)
            for p in range(2):
                X = (1 + p) if dr < 0 else (27 + p)
                for h in range(2):
                    for j in range(2):
                        v = vrecv[n, (p * 2 + h) * 2 + j] * side
                        if db < 0:
                            UB[X, h, 2 + j, 0:1, :] = v
                        else:
                            UB[X, h, 5 + j, 7:8, :] = v

    for cp in rmsg:
        cp.wait()

    def solve():
        msgs = [RM[:, i] for i in range(3)]
        res = gather([m[1:16] for m in msgs], 0)
        face = gather([m[1:16] for m in msgs], 1)
        res = res + jnp.where(sub == 0, down_y(face), jnp.where(sub == 7, up_y(face), 0.0))
        face = gather(msgs, 2)
        start = []
        for s in range(15):
            v = res[s]
            if s % 3 == 0:
                v = v + face[s]
            if s % 3 == 2:
                v = v + face[s + 2]
            v = CO[s, 0] * v
            RO[s] = v
            start.append(v)
        e = dict(enumerate(start))
        for it in range(1, 6):
            new = {}
            for s in range(it, 15 - it):
                v = e[s]
                off = CO[s, 1] * e[s - 1] + CO[s, 2] * e[s + 1]
                off = off + CO[s, 3] * down_y(v) + CO[s, 4] * up_y(v)
                off = off + CO[s, 5] * pltpu.roll(v, 1, 1) + CO[s, 6] * pltpu.roll(v, 127, 1)
                new[s] = 0.2 * v + (RO[s] + off)
            e = new
        parts = []
        for s in range(5, 10):
            parts += [e[s], down_y(e[s]), up_y(e[s])]
        wide[...] = dot(jnp.concatenate(parts, axis=0), px[...])

    solve()

    for cp in uxmsg:
        cp.wait_recv()
    for cp in ucmsg:
        cp.wait()
    u_halo()

    for s in range(5):
        for h in range(2):
            mid, dn, up = (wide[24 * s + 8 * i : 24 * s + 8 * i + 8, 128 * h : 128 * h + 128] for i in range(3))
            lay = []
            for i in range(YV):
                v = mid
                if i < 4:
                    v = jnp.where(sub < 4 - i, dn, v)
                elif i > 4:
                    v = jnp.where(sub >= 12 - i, up, v)
                lay.append(v)
            lay = jnp.stack(lay, axis=0)
            LAY[s, h] = lay

    def add(X):
        for h in range(2):
            UA[X, h] = UB[X, h] + cs[X, h] * LAY[lax.div(X + 5, 8), h]

    def third(X):
        add(X + 1)
        for h, v in enumerate(sweep(UA, X)):
            UC[X, h] = v

    def fourth(X):
        for h, v in enumerate(sweep(UC, X)):
            UA[X, h] = v

    def fifth(X):
        for h, v in enumerate(sweep(UA, X)):
            v = v * RC[X, h]
            for i in range(YV):
                on[X - XO, h, pl.ds(4 + i, 8, stride=9), :] = v[i]
            out_ref[X - XO, :, 128 * h : 128 * h + 128] = on[X - XO, h, 8:72, :]

    add(0)
    add(1)
    run(third, -2, 26, 14)
    run(fourth, -1, 25, 26)
    run(fifth, 0, XL, 24)


def vmem(*shape):
    return pltpu.VMEM(shape, F32)


def shards(right_side, knudsen, solid):
    n_msg = 2 * NCH + 8 + 20 + 14 + 8
    scratch = [
        vmem(XL, 64, 256), pltpu.VMEM((XL, 64, 256), jnp.int32), vmem(30, 2, 80, 128), vmem(28, 2, 80, 128),
    ]
    scratch += [vmem(30, 2, YV, 8, 128) for _ in range(7)]
    scratch += [vmem(XL, 2, 80, 128)]
    scratch += [vmem(2, NCH, CH * 10, 1, 128), vmem(2, NCH, CH * 10, 1, 128), vmem(4, 10, 1, 128), vmem(4, 10, 1, 128)]
    scratch += [vmem(2, 144, 1, 128), vmem(2, 144, 1, 128), vmem(4, 8, 1, 128), vmem(4, 8, 1, 128)]
    scratch += [vmem(2, 3, 2, YV, 8, 128)]
    scratch += [
        vmem(3, 2, YV, 8, 128), vmem(3, 2, 8, 128), vmem(3, 2, YV, 8, 128), vmem(3, 2, YV, 8, 128),
        vmem(3, 2, YV, 8, 128), vmem(3, 2, 8, 128),
    ]
    scratch += [vmem(15, 3, 8, 128), vmem(17, 3, 8, 128), vmem(15, 7, 8, 128), vmem(15, 8, 128)]
    scratch += [vmem(256, 128), vmem(128, 256), vmem(256, 128), vmem(XL, 64, 256), vmem(11, 8, 128), vmem(120, 256), vmem(5, 2, YV, 8, 128), vmem(30, 2, YV, 8, 128)]
    scratch += [
        pltpu.SemaphoreType.DMA((3 * NCH,)),
        pltpu.SemaphoreType.DMA((n_msg,)), pltpu.SemaphoreType.DMA((n_msg,)),
    ]
    return pl.pallas_call(
        kernel,
        name="vcycle",
        out_shape=pltpu.VMEM(right_side.shape, F32),
        in_specs=[pl.BlockSpec(memory_space=pltpu.HBM)] * 3,
        out_specs=pl.BlockSpec(memory_space=pltpu.VMEM),
        scratch_shapes=scratch,
        compiler_params=pltpu.CompilerParams(
            collective_id=0, has_side_effects=True, vmem_limit_bytes=58 * 2**20
        ),
    )(knudsen, solid, right_side)


def solution(mesh):
    placed = P("region", "block", None)
    return jax.shard_map(shards, mesh=mesh, in_specs=(placed,) * 3, out_specs=placed, check_vma=False)
```
